512 devices in a mesh: bucket: 128 (over x, z_lo, y), rel: 4 (over z_hi, core).
Axes of the slice: x: 4, y: 8, z: 8 (z_hi: 2, z_lo: 4; z = z_hi * 4 + z_lo), core: 2. Of those that a mesh axis runs over, the one named last changes fastest.
Arguments:
- src_feat: bfloat16 [32768, 768], P(('bucket', 'rel')), may hold values from -22 to 22
- tgt_feat: bfloat16 [65536, 768], P(('bucket', 'rel')), may hold values from -22 to 22
- enc_weight: bfloat16 [768, 512], replicated, may hold values from -0.21875 to 0.21875
- rel_shift: bfloat16 [12, 512], P('rel'), may hold values from -3 to 3
- edge_src: int32 [128, 4, 4, 768], P('bucket', 'rel'), may hold values from 0 to 255
- edge_tgt: int32 [128, 4, 4, 768], P('bucket', 'rel'), may hold values from 0 to 511
- rel_hot: int32 [128, 4, 4, 3, 768], P('bucket', 'rel'), may hold values from 0 to 1, as said below
- neg_idx: int32 [128, 4, 4, 128], P('bucket', 'rel'), may hold values from 0 to 511
- edge_label: int32 [128, 4, 4, 768], P('bucket', 'rel'), may hold values 0 or 1
Outputs:
- src_grad: float32 [32768, 512], P(('bucket', 'rel'))
- tgt_grad: float32 [65536, 512], P(('bucket', 'rel'))
- rel_grad: float32 [12, 512], P('rel')
- enc_grad: float32 [768, 512], replicated
The draws below stay inside these ranges and needn't reach their ends.
Inputs may be any that keep to these rules, and one draw needn't show every extreme that they name: `rel_hot`: for each edge exactly one of the three entries is 1.
All inputs are finite; a program needn't handle non-finite values. No bound on the sum of `edge_label` on one device may be relied on, other than what follows from the above.
Results may differ from the reference program's by a relative error of at most 0.00065.
The reference program's roundings to bfloat16 on the way (of `src_emb`, `tgt_emb` and `query`) count: a program that leaves them out, or rounds other values in their place, can miss the bound.
Values may be sent and summed in bfloat16 or wider, within the bound.
A program may use at most 64 MiB of HBM per device.

```python
import jax
import jax.numpy as jnp
from jax import lax

F = 768
EMB = 512
SRC_DEV = 256
TGT_DEV = 512
EDGES = 768
NEG = 128
MEETS = 4
BUCKETS = 128
GROUPS = 4
NSRC = 32768
NTGT = 65536


def draw_rel_hot(key, part):
    which = jax.random.randint(jax.random.fold_in(key, 17), (BUCKETS, GROUPS, MEETS, EDGES), 0, 3)
    levels = jnp.arange(3, dtype=jnp.int32)
    return (which[:, :, :, None, :] == levels[None, None, None, :, None]).astype(jnp.int32)


def shared_directions(key):
    base = jax.random.fold_in(key, 7)
    return jnp.clip(jax.random.normal(base, (2, F), jnp.float32), -3.0, 3.0)


def block_spike(key, row_count, salt):
    block_count = BUCKETS * GROUPS
    rows_block = row_count // block_count
    columns = jax.random.randint(jax.random.fold_in(key, salt + 100), (block_count,), 0, F)
    picked = (columns[:, None] == jnp.arange(F, dtype=jnp.int32)[None, :]).astype(jnp.float32)
    factor = 1.0 + 2.0 * picked
    return jnp.repeat(factor, rows_block, axis=0)


def node_features(key, row_count, salt):
    directions = shared_directions(key)
    node_key = jax.random.fold_in(key, salt)
    key_noise, key_coef = jax.random.split(node_key, 2)
    noise = jnp.clip(jax.random.normal(key_noise, (row_count, F), jnp.float32), -4.0, 4.0)
    coef = 0.5 * jnp.clip(jax.random.normal(key_coef, (row_count, 2), jnp.float32), -3.0, 3.0)
    feats = noise + coef[:, 0:1] * directions[0][None, :] + coef[:, 1:2] * directions[1][None, :]
    feats = feats * block_spike(key, row_count, salt)
    return feats.astype(jnp.bfloat16)


def draw_src_feat(key, part):
    return node_features(key, NSRC, 11)


def draw_tgt_feat(key, part):
    return node_features(key, NTGT, 13)


def place_ends(entries, stream_key, least, high):
    place = [jax.random.randint(jax.random.fold_in(stream_key, axis), (), 0, length) for axis, length in enumerate(entries.shape)]
    longest = entries.shape.index(max(entries.shape))
    neighbour = place[:longest] + [(place[longest] + 1) % entries.shape[longest]] + place[longest + 1:]
    return entries.at[tuple(place)].set(least).at[tuple(neighbour)].set(high)


def steps_of(key, extent, pieces, smallest, top_value):
    gain, own = 1.0, jax.random.fold_in(key, 6)
    for dim, blocks in pieces:
        heights = jnp.exp(jax.random.uniform(jax.random.fold_in(own, dim), (blocks,), jnp.float32, smallest / len(pieces), top_value / len(pieces)))
        gain = gain * jnp.repeat(heights, extent[dim] // blocks).reshape([-1 if axis == dim else 1 for axis in range(len(extent))])
    return gain


def centred(stream_key, shape, scale, limit, cuts=(), kind=jnp.bfloat16):
    gain = steps_of(stream_key, shape, cuts, -0.22, 0.18) if cuts else 1.0
    entries = jax.random.normal(stream_key, shape, jnp.float32) * scale * gain
    return jnp.minimum(jnp.maximum(entries, -limit), limit).astype(kind)


def setup_inputs(seed: int = 0) -> dict:
    splits = jax.random.split(jax.random.key(seed), 10)
    src_feat = draw_src_feat(jax.random.fold_in(splits[9], 71), 0)
    tgt_feat = draw_tgt_feat(jax.random.fold_in(splits[9], 71), 0)
    enc_weight = centred(splits[2], (F, EMB), F ** -0.5, 0.21875)
    rel_shift = centred(splits[3], (GROUPS * 3, EMB), 0.5, 3.0, ((0, 4),))
    edge_src = place_ends(jax.random.randint(splits[4], (BUCKETS, GROUPS, MEETS, EDGES), 0, SRC_DEV), jax.random.fold_in(splits[4], 1), 0, SRC_DEV - 1).astype(jnp.int32)
    edge_tgt = place_ends(jax.random.randint(splits[5], (BUCKETS, GROUPS, MEETS, EDGES), 0, TGT_DEV), jax.random.fold_in(splits[5], 1), 0, TGT_DEV - 1).astype(jnp.int32)
    rel_hot = draw_rel_hot(jax.random.fold_in(splits[9], 71), 0)
    neg_idx = place_ends(jax.random.randint(splits[7], (BUCKETS, GROUPS, MEETS, NEG), 0, TGT_DEV), jax.random.fold_in(splits[7], 1), 0, TGT_DEV - 1).astype(jnp.int32)
    edge_label = place_ends((jax.random.randint(splits[8], (BUCKETS, GROUPS, MEETS, EDGES), 0, 2) < 1).astype(jnp.int32), jax.random.fold_in(splits[8], 1), 0, 1)
    return dict(src_feat=src_feat, tgt_feat=tgt_feat, enc_weight=enc_weight, rel_shift=rel_shift, edge_src=edge_src, edge_tgt=edge_tgt, rel_hot=rel_hot, neg_idx=neg_idx, edge_label=edge_label)


def meet(source, block, shifts, src_ids, tgt_ids, hot, neg_ids, label):
    scale = EMB ** -0.5
    hot_b = hot.astype(jnp.bfloat16)
    shift = jnp.einsum("ke,kd->ed", hot_b, shifts, preferred_element_type=jnp.float32)
    query = (source[src_ids].astype(jnp.float32) + shift).astype(jnp.bfloat16)
    query_f = query.astype(jnp.float32)
    pos_rows = block[tgt_ids]
    neg_rows = block[neg_ids]
    pos = scale * jnp.sum(query_f * pos_rows.astype(jnp.float32), axis=1)
    neg = scale * jnp.einsum("ed,nd->en", query, neg_rows, preferred_element_type=jnp.float32)
    grad_pos = jax.nn.sigmoid(pos) - label.astype(jnp.float32)
    grad_neg = (jax.nn.sigmoid(neg) / NEG).astype(jnp.bfloat16)
    d_query = scale * (grad_pos[:, None] * pos_rows.astype(jnp.float32)
                       + jnp.einsum("en,nd->ed", grad_neg, neg_rows, preferred_element_type=jnp.float32))
    src_part = jnp.zeros((source.shape[0], EMB), jnp.float32).at[src_ids].add(d_query)
    tgt_part = jnp.zeros((block.shape[0], EMB), jnp.float32).at[tgt_ids].add(scale * grad_pos[:, None] * query_f)
    tgt_part = tgt_part.at[neg_ids].add(scale * jnp.einsum("en,ed->nd", grad_neg, query, preferred_element_type=jnp.float32))
    rel_part = jnp.einsum("ke,ed->kd", hot.astype(jnp.float32), d_query, precision=lax.Precision.HIGHEST)
    return src_part, tgt_part, rel_part


def reference(src_feat, tgt_feat, enc_weight, rel_shift, edge_src, edge_tgt, rel_hot, neg_idx, edge_label):
    src_act = jnp.tanh(jnp.dot(src_feat, enc_weight, preferred_element_type=jnp.float32))
    tgt_act = jnp.tanh(jnp.dot(tgt_feat, enc_weight, preferred_element_type=jnp.float32))
    src_emb = src_act.astype(jnp.bfloat16)
    tgt_emb = tgt_act.astype(jnp.bfloat16)
    half = BUCKETS // 2
    masks = [0, 1, 1 + half, half]

    def one_pair(flat, carry):
        src_total, tgt_total, rel_total = carry
        bucket = flat // GROUPS
        group = flat % GROUPS
        source = lax.dynamic_slice_in_dim(src_emb, (bucket * SRC_DEV).astype(jnp.int32), SRC_DEV, 0)
        shifts = lax.dynamic_slice_in_dim(rel_shift, (group * 3).astype(jnp.int32), 3, 0)
        src_sum = jnp.zeros((SRC_DEV, EMB), jnp.float32)
        rel_sum = jnp.zeros((3, EMB), jnp.float32)
        for slot in range(MEETS):
            partner = jnp.bitwise_xor(bucket, masks[slot]).astype(jnp.int32)
            block = lax.dynamic_slice_in_dim(tgt_emb, partner * TGT_DEV, TGT_DEV, 0)
            src_part, tgt_part, rel_part = meet(source, block, shifts, edge_src[bucket, group, slot],
                                               edge_tgt[bucket, group, slot], rel_hot[bucket, group, slot],
                                               neg_idx[bucket, group, slot], edge_label[bucket, group, slot])
            src_sum = src_sum + src_part
            rel_sum = rel_sum + rel_part
            old = lax.dynamic_slice_in_dim(tgt_total, partner * TGT_DEV, TGT_DEV, 0)
            tgt_total = lax.dynamic_update_slice_in_dim(tgt_total, old + tgt_part, partner * TGT_DEV, 0)
        old_src = lax.dynamic_slice_in_dim(src_total, (bucket * SRC_DEV).astype(jnp.int32), SRC_DEV, 0)
        src_total = lax.dynamic_update_slice_in_dim(src_total, old_src + src_sum, (bucket * SRC_DEV).astype(jnp.int32), 0)
        old_rel = lax.dynamic_slice_in_dim(rel_total, (group * 3).astype(jnp.int32), 3, 0)
        rel_total = lax.dynamic_update_slice_in_dim(rel_total, old_rel + rel_sum, (group * 3).astype(jnp.int32), 0)
        return src_total, tgt_total, rel_total

    start = (jnp.zeros((NSRC, EMB), jnp.float32), jnp.zeros((NTGT, EMB), jnp.float32),
             jnp.zeros((GROUPS * 3, EMB), jnp.float32))
    src_grad, tgt_grad, rel_grad = lax.fori_loop(0, BUCKETS * GROUPS, one_pair, start)
    d_src = (src_grad * (1.0 - src_act * src_act)).astype(jnp.bfloat16)
    d_tgt = (tgt_grad * (1.0 - tgt_act * tgt_act)).astype(jnp.bfloat16)
    enc_grad = (jnp.einsum("rf,re->fe", src_feat, d_src, preferred_element_type=jnp.float32)
                + jnp.einsum("rf,re->fe", tgt_feat, d_tgt, preferred_element_type=jnp.float32))
    return src_grad, tgt_grad, rel_grad, enc_grad
```

```python
import jax
import jax.numpy as jnp
from jax import lax
from jax.experimental import pallas as pl
from jax.experimental.pallas import tpu as pltpu
from jax.sharding import PartitionSpec as P

EMB = 512
NEG = 128
MEETS = 4
F32 = jnp.float32
BF16 = jnp.bfloat16
MESH = pl.DeviceIdType.MESH
AXIS = {"x": 4, "y": 8, "z": 8}
HALF = 224
PARTS = (("z", "y", "x", 0, 64), ("y", "z", "x", 64, 64), ("x", "y", "z", 128, 96))


class Place:
    def __init__(self):
        b, q = lax.axis_index("bucket"), lax.axis_index("rel")
        self.at = {
            "x": lax.div(b, 32),
            "y": lax.rem(b, 8),
            "z": lax.div(q, 2) * 4 + lax.rem(lax.div(b, 8), 4),
            "k": lax.rem(q, 2),
        }

    def device(self, **moved):
        at = dict(self.at, **moved)
        bucket = at["x"] * 32 + lax.rem(at["z"], 4) * 8 + at["y"]
        return bucket, lax.div(at["z"], 4) * 2 + at["k"]

    def along(self, axis, apart):
        there = lax.rem(self.at[axis] + apart, AXIS[axis])
        return there, self.device(**{axis: there})

    def other_core(self):
        return self.device(k=1 - self.at["k"])


class Wires:
    def __init__(self, send_sems, recv_sems):
        self.send_sems, self.recv_sems, self.used, self.open = send_sems, recv_sems, 0, []

    def send(self, src, dst, device):
        copy = pltpu.make_async_remote_copy(
            src_ref=src,
            dst_ref=dst,
            send_sem=self.send_sems.at[self.used],
            recv_sem=self.recv_sems.at[self.used],
            device_id=device,
            device_id_type=MESH,
        )
        copy.start()
        self.used += 1
        self.open.append(copy)
        return copy

    def finish(self):
        for copy in self.open:
            copy.wait_send()


def reduce_everywhere(place, wires, local, pair, mine, full, firsts, seconds, thirds, sums1, sums2):
    at, k = place.at, place.at["k"]
    other = place.other_core()
    copies = []
    for _, _, _, base, size in PARTS:
        size = min(size, 196 - base)
        copies.append(
            wires.send(local.at[pl.ds((1 - k) * HALF + base, size)], pair.at[pl.ds(base, size)], other)
        )
    mine[pl.ds(196, 28)] = jnp.zeros((28, 8, 128), F32)
    pending1 = []
    for p, (first, _, _, base, size) in enumerate(PARTS):
        copies[p].wait_recv()
        real = min(size, 196 - base)
        mine[pl.ds(base, real)] = local[pl.ds(k * HALF + base, real)] + pair[pl.ds(base, real)]
        block = size // AXIS[first]
        here = []
        for apart in range(1, AXIS[first]):
            there, device = place.along(first, apart)
            here.append(
                wires.send(mine.at[pl.ds(base + there * block, block)], firsts[p].at[apart], device)
            )
        pending1.append(here)
    pending2 = []
    for p, (first, second, _, base, size) in enumerate(PARTS):
        block = size // AXIS[first]
        total = mine[pl.ds(base + at[first] * block, block)]
        for apart in range(1, AXIS[first]):
            pending1[p][apart - 1].wait_recv()
            total = total + firsts[p][apart]
        sums1[p][...] = total
        small = block // AXIS[second]
        here = []
        for apart in range(1, AXIS[second]):
            there, device = place.along(second, apart)
            here.append(
                wires.send(sums1[p].at[pl.ds(there * small, small)], seconds[p].at[apart], device)
            )
        pending2.append(here)
    pending3 = []
    for p, (first, second, third, base, size) in enumerate(PARTS):
        small = size // AXIS[first] // AXIS[second]
        total = sums1[p][pl.ds(at[second] * small, small)]
        for apart in range(1, AXIS[second]):
            pending2[p][apart - 1].wait_recv()
            total = total + seconds[p][apart]
        sums2[p][...] = total
        here = []
        for apart in range(1, AXIS[third]):
            here.append(wires.send(sums2[p], thirds[p].at[apart], place.along(third, apart)[1]))
        pending3.append(here)
    pending4 = []
    for p, (first, second, third, base, size) in enumerate(PARTS):
        thirds[p][0] = sums2[p][...]
        for apart in range(1, AXIS[third]):
            pending3[p][apart - 1].wait_recv()
        total = 0.0
        for where in range(AXIS[third]):
            total = total + thirds[p][lax.rem(at[third] + AXIS[third] - where, AXIS[third])]
        block = size // AXIS[first]
        small = block // AXIS[second]
        own = k * HALF + base + at[first] * block + at[second] * small
        full[pl.ds(own, small)] = total
        here = []
        for apart in range(1, AXIS[second]):
            piece = full.at[pl.ds(own, small)]
            here.append(wires.send(piece, piece, place.along(second, apart)[1]))
        pending4.append(here)
    pending5, pending6 = [], []
    for p, (first, second, third, base, size) in enumerate(PARTS):
        block = size // AXIS[first]
        for copy in pending4[p]:
            copy.wait_recv()
        piece = full.at[pl.ds(k * HALF + base + at[first] * block, block)]
        pending5.append(
            [wires.send(piece, piece, place.along(first, apart)[1]) for apart in range(1, AXIS[first])]
        )
        pending6.append(wires.send(piece, piece, other))
    for p, (first, second, third, base, size) in enumerate(PARTS):
        block = size // AXIS[first]
        for apart in range(1, AXIS[first]):
            pending5[p][apart - 1].wait_recv()
            start = lax.rem(at[first] + AXIS[first] - apart, AXIS[first])
            piece = full.at[pl.ds(k * HALF + base + start * block, block)]
            pending6.append(wires.send(piece, piece, other))
    for copy in pending6:
        copy.wait_recv()


WIRES = 3 + 17 + 21 + 13 + 21 + 17 + 20


def scratch_of_reduce():
    tile = (8, 128)
    firsts = [pltpu.VMEM((AXIS[f], n // AXIS[f]) + tile, F32) for f, s, t, _, n in PARTS]
    small = [n // AXIS[f] // AXIS[s] for f, s, t, _, n in PARTS]
    seconds = [pltpu.VMEM((AXIS[p[1]], m) + tile, F32) for p, m in zip(PARTS, small)]
    thirds = [pltpu.VMEM((AXIS[p[2]], m) + tile, F32) for p, m in zip(PARTS, small)]
    sums1 = [pltpu.VMEM((n // AXIS[f],) + tile, F32) for f, s, t, _, n in PARTS]
    sums2 = [pltpu.VMEM((m,) + tile, F32) for m in small]
    return [
        pltpu.VMEM((2 * HALF,) + tile, F32),
        pltpu.VMEM((HALF,) + tile, F32),
        pltpu.VMEM((HALF,) + tile, F32),
        pltpu.VMEM((2 * HALF,) + tile, F32),
        firsts,
        seconds,
        thirds,
        sums1,
        sums2,
    ]


def greet(place, barrier, devices):
    for device in devices:
        pl.semaphore_signal(barrier, inc=1, device_id=device, device_id_type=MESH)


def tiles_in(local, enc, rel):
    for column in range(4):
        half, low = column // 2 * HALF, column % 2
        tiles = enc[:, column * 128 : column * 128 + 128].reshape(96, 8, 128)
        local[half + low * 96 : half + low * 96 + 96] = tiles
        tiles = rel[:, column * 128 : column * 128 + 128].reshape(2, 8, 128)
        local[half + 192 + low * 2 : half + 194 + low * 2] = tiles


def tiles_out(full, enc_ref, rel_ref):
    g = lax.axis_index("rel")
    for column in range(4):
        half, low = column // 2 * HALF, column % 2
        lanes = pl.ds(column * 128, 128)
        enc_ref[:, lanes] = full[half + low * 96 : half + low * 96 + 96].reshape(768, 128)
        rows = full[half + 192 + low * 2 : half + 194 + low * 2].reshape(16, 128)
        part = jnp.zeros((3, 128), F32)
        for group in range(4):
            part = jnp.where(g == group, rows[group * 3 : group * 3 + 3], part)
        rel_ref[:, lanes] = part


def reduce_kernel(enc_ref, rel_ref, enc_out, rel_out, *scratch):
    *buffers, send_sems, recv_sems = scratch
    place = Place()
    barrier = pltpu.get_barrier_semaphore()
    others = [place.along(axis, apart)[1] for axis, n in AXIS.items() for apart in range(1, n)]
    others.append(place.other_core())
    greet(place, barrier, others)
    tiles_in(buffers[0], enc_ref[...], rel_ref[...])
    pl.semaphore_wait(barrier, len(others))
    wires = Wires(send_sems, recv_sems)
    reduce_everywhere(place, wires, *buffers)
    tiles_out(buffers[3], enc_out, rel_out)
    wires.finish()


def summed(enc, rel):
    return pl.pallas_call(
        reduce_kernel,
        out_shape=(jax.ShapeDtypeStruct((768, EMB), F32), jax.ShapeDtypeStruct((3, EMB), F32)),
        in_specs=[pl.BlockSpec(memory_space=pltpu.VMEM)] * 2,
        out_specs=(pl.BlockSpec(memory_space=pltpu.VMEM),) * 2,
        scratch_shapes=scratch_of_reduce()
        + [pltpu.SemaphoreType.DMA((WIRES,)), pltpu.SemaphoreType.DMA((WIRES,))],
        compiler_params=pltpu.CompilerParams(
            collective_id=0, has_side_effects=True, vmem_limit_bytes=40 * 2**20
        ),
    )(enc, rel)


def swapped(array, axis, apart):
    return lax.ppermute(array, axis, [(i, i ^ 1 << apart) for i in range(lax.axis_size(axis))])


def meet(source, block, shifts, src_ids, tgt_ids, hot, neg_ids, label):
    scale = EMB ** (-0.5)
    hot_b = hot.astype(jnp.bfloat16)
    shift = jnp.einsum("ke,kd->ed", hot_b, shifts, preferred_element_type=jnp.float32)
    query = (source[src_ids].astype(jnp.float32) + shift).astype(jnp.bfloat16)
    query_f = query.astype(jnp.float32)
    pos_rows = block[tgt_ids]
    neg_rows = block[neg_ids]
    pos = scale * jnp.sum(query_f * pos_rows.astype(jnp.float32), axis=1)
    neg = scale * jnp.einsum("ed,nd->en", query, neg_rows, preferred_element_type=jnp.float32)
    grad_pos = jax.nn.sigmoid(pos) - label.astype(jnp.float32)
    grad_neg = (jax.nn.sigmoid(neg) / NEG).astype(jnp.bfloat16)
    d_query = scale * (
        grad_pos[:, None] * pos_rows.astype(jnp.float32)
        + jnp.einsum("en,nd->ed", grad_neg, neg_rows, preferred_element_type=jnp.float32)
    )
    src_part = jnp.zeros((source.shape[0], EMB), jnp.float32).at[src_ids].add(d_query)
    tgt_part = (
        jnp.zeros((block.shape[0], EMB), jnp.float32)
        .at[tgt_ids]
        .add(scale * grad_pos[:, None] * query_f)
    )
    tgt_part = tgt_part.at[neg_ids].add(
        scale * jnp.einsum("en,ed->nd", grad_neg, query, preferred_element_type=jnp.float32)
    )
    rel_part = jnp.einsum(
        "ke,ed->kd", hot.astype(jnp.float32), d_query, precision=lax.Precision.HIGHEST
    )
    return (src_part, tgt_part, rel_part)


def shards(
    src_feat, tgt_feat, enc_weight, rel_shift, edge_src, edge_tgt, rel_hot, neg_idx, edge_label
):
    src_act = jnp.tanh(jnp.dot(src_feat, enc_weight, preferred_element_type=jnp.float32))
    tgt_act = jnp.tanh(jnp.dot(tgt_feat, enc_weight, preferred_element_type=jnp.float32))
    source, home_block = (
        lax.all_gather(src_act.astype(jnp.bfloat16), "rel", axis=0, tiled=True),
        lax.all_gather(tgt_act.astype(jnp.bfloat16), "rel", axis=0, tiled=True),
    )
    high_bit = lax.axis_size("bucket").bit_length() - 2
    slots = [0, 1, 2, 3]
    bits = [0, high_bit, 0]
    src_sum = jnp.zeros((source.shape[0], EMB), jnp.float32)
    rel_sum = jnp.zeros((3, EMB), jnp.float32)
    block = home_block
    carried = jnp.zeros((block.shape[0], EMB), jnp.float32)
    for step in range(MEETS):
        if step > 0:
            block, carried = (
                swapped(block.astype(jnp.float32), "bucket", bits[step - 1]).astype(block.dtype),
                swapped(carried, "bucket", bits[step - 1]),
            )
        slot = slots[step]
        src_part, tgt_part, rel_part = meet(
            source,
            block,
            rel_shift,
            edge_src[0, 0, slot],
            edge_tgt[0, 0, slot],
            rel_hot[0, 0, slot],
            neg_idx[0, 0, slot],
            edge_label[0, 0, slot],
        )
        src_sum = src_sum + src_part
        rel_sum = rel_sum + rel_part
        carried = carried + tgt_part
    tgt_sum = swapped(carried, "bucket", high_bit)
    src_grad, tgt_grad = (
        lax.psum_scatter(src_sum, "rel", scatter_dimension=0, tiled=True),
        lax.psum_scatter(tgt_sum, "rel", scatter_dimension=0, tiled=True),
    )
    d_src = (src_grad * (1.0 - src_act * src_act)).astype(jnp.bfloat16)
    d_tgt = (tgt_grad * (1.0 - tgt_act * tgt_act)).astype(jnp.bfloat16)
    enc_local = jnp.einsum(
        "rf,re->fe", src_feat, d_src, preferred_element_type=jnp.float32
    ) + jnp.einsum("rf,re->fe", tgt_feat, d_tgt, preferred_element_type=jnp.float32)
    rel_all = lax.dynamic_update_slice(
        jnp.zeros((16, EMB), F32), rel_sum, (lax.axis_index("rel") * 3, 0)
    )
    enc_grad, rel_grad = summed(enc_local, rel_all)
    return (src_grad, tgt_grad, rel_grad, enc_grad)


def solution(mesh):
    in_specs = (
        P(("bucket", "rel"), None),
        P(("bucket", "rel"), None),
        P(),
        P("rel", None),
        P("bucket", "rel", None, None),
        P("bucket", "rel", None, None),
        P("bucket", "rel", None, None, None),
        P("bucket", "rel", None, None),
        P("bucket", "rel", None, None),
    )
    out_specs = (P(("bucket", "rel"), None), P(("bucket", "rel"), None), P("rel", None), P())
    return jax.shard_map(shards, mesh=mesh, in_specs=in_specs, out_specs=out_specs, check_vma=False)
```

```python
import jax
import jax.numpy as jnp
from jax import lax
from jax.experimental import pallas as pl
from jax.experimental.pallas import tpu as pltpu
from jax.sharding import PartitionSpec as P

EMB = 512
NEG = 128
MEETS = 4
F32 = jnp.float32
BF16 = jnp.bfloat16
MESH = pl.DeviceIdType.MESH
AXIS = {"x": 4, "y": 8, "z": 8}
HALF = 224
PARTS = (("z", "y", "x", 0, 64), ("y", "z", "x", 64, 64), ("x", "y", "z", 128, 96))


class Place:
    def __init__(self):
        b, q = lax.axis_index("bucket"), lax.axis_index("rel")
        self.at = {
            "x": lax.div(b, 32),
            "y": lax.rem(b, 8),
            "z": lax.div(q, 2) * 4 + lax.rem(lax.div(b, 8), 4),
            "k": lax.rem(q, 2),
        }

    def device(self, **moved):
        at = dict(self.at, **moved)
        bucket = at["x"] * 32 + lax.rem(at["z"], 4) * 8 + at["y"]
        return bucket, lax.div(at["z"], 4) * 2 + at["k"]

    def along(self, axis, apart):
        there = lax.rem(self.at[axis] + apart, AXIS[axis])
        return there, self.device(**{axis: there})

    def other_core(self):
        return self.device(k=1 - self.at["k"])


class Wires:
    def __init__(self, send_sems, recv_sems):
        self.send_sems, self.recv_sems, self.used, self.open = send_sems, recv_sems, 0, []

    def send(self, src, dst, device):
        copy = pltpu.make_async_remote_copy(
            src_ref=src,
            dst_ref=dst,
            send_sem=self.send_sems.at[self.used],
            recv_sem=self.recv_sems.at[self.used],
            device_id=device,
            device_id_type=MESH,
        )
        copy.start()
        self.used += 1
        self.open.append(copy)
        return copy

    def finish(self):
        for copy in self.open:
            copy.wait_send()


def reduce_everywhere(place, wires, local, pair, mine, full, firsts, seconds, thirds, sums1, sums2):
    at, k = place.at, place.at["k"]
    other = place.other_core()
    copies = []
    for _, _, _, base, size in PARTS:
        size = min(size, 196 - base)
        copies.append(
            wires.send(local.at[pl.ds((1 - k) * HALF + base, size)], pair.at[pl.ds(base, size)], other)
        )
    mine[pl.ds(196, 28)] = jnp.zeros((28, 8, 128), F32)
    pending1 = []
    for p, (first, _, _, base, size) in enumerate(PARTS):
        copies[p].wait_recv()
        real = min(size, 196 - base)
        mine[pl.ds(base, real)] = local[pl.ds(k * HALF + base, real)] + pair[pl.ds(base, real)]
        block = size // AXIS[first]
        here = []
        for apart in range(1, AXIS[first]):
            there, device = place.along(first, apart)
            here.append(
                wires.send(mine.at[pl.ds(base + there * block, block)], firsts[p].at[apart], device)
            )
        pending1.append(here)
    pending2 = []
    for p, (first, second, _, base, size) in enumerate(PARTS):
        block = size // AXIS[first]
        total = mine[pl.ds(base + at[first] * block, block)]
        for apart in range(1, AXIS[first]):
            pending1[p][apart - 1].wait_recv()
            total = total + firsts[p][apart]
        sums1[p][...] = total
        small = block // AXIS[second]
        here = []
        for apart in range(1, AXIS[second]):
            there, device = place.along(second, apart)
            here.append(
                wires.send(sums1[p].at[pl.ds(there * small, small)], seconds[p].at[apart], device)
            )
        pending2.append(here)
    pending3 = []
    for p, (first, second, third, base, size) in enumerate(PARTS):
        small = size // AXIS[first] // AXIS[second]
        total = sums1[p][pl.ds(at[second] * small, small)]
        for apart in range(1, AXIS[second]):
            pending2[p][apart - 1].wait_recv()
            total = total + seconds[p][apart]
        sums2[p][...] = total
        here = []
        for apart in range(1, AXIS[third]):
            here.append(wires.send(sums2[p], thirds[p].at[apart], place.along(third, apart)[1]))
        pending3.append(here)
    pending4 = []
    for p, (first, second, third, base, size) in enumerate(PARTS):
        thirds[p][0] = sums2[p][...]
        for apart in range(1, AXIS[third]):
            pending3[p][apart - 1].wait_recv()
        total = 0.0
        for where in range(AXIS[third]):
            total = total + thirds[p][lax.rem(at[third] + AXIS[third] - where, AXIS[third])]
        block = size // AXIS[first]
        small = block // AXIS[second]
        own = k * HALF + base + at[first] * block + at[second] * small
        full[pl.ds(own, small)] = total
        here = []
        for apart in range(1, AXIS[second]):
            piece = full.at[pl.ds(own, small)]
            here.append(wires.send(piece, piece, place.along(second, apart)[1]))
        pending4.append(here)
    pending5, pending6 = [], []
    for p, (first, second, third, base, size) in enumerate(PARTS):
        block = size // AXIS[first]
        for copy in pending4[p]:
            copy.wait_recv()
        piece = full.at[pl.ds(k * HALF + base + at[first] * block, block)]
        pending5.append(
            [wires.send(piece, piece, place.along(first, apart)[1]) for apart in range(1, AXIS[first])]
        )
        pending6.append(wires.send(piece, piece, other))
    for p, (first, second, third, base, size) in enumerate(PARTS):
        block = size // AXIS[first]
        for apart in range(1, AXIS[first]):
            pending5[p][apart - 1].wait_recv()
            start = lax.rem(at[first] + AXIS[first] - apart, AXIS[first])
            piece = full.at[pl.ds(k * HALF + base + start * block, block)]
            pending6.append(wires.send(piece, piece, other))
    for copy in pending6:
        copy.wait_recv()


WIRES = 3 + 17 + 21 + 13 + 21 + 17 + 20


def scratch_of_reduce():
    tile = (8, 128)
    firsts = [pltpu.VMEM((AXIS[f], n // AXIS[f]) + tile, F32) for f, s, t, _, n in PARTS]
    small = [n // AXIS[f] // AXIS[s] for f, s, t, _, n in PARTS]
    seconds = [pltpu.VMEM((AXIS[p[1]], m) + tile, F32) for p, m in zip(PARTS, small)]
    thirds = [pltpu.VMEM((AXIS[p[2]], m) + tile, F32) for p, m in zip(PARTS, small)]
    sums1 = [pltpu.VMEM((n // AXIS[f],) + tile, F32) for f, s, t, _, n in PARTS]
    sums2 = [pltpu.VMEM((m,) + tile, F32) for m in small]
    return [
        pltpu.VMEM((2 * HALF,) + tile, F32),
        pltpu.VMEM((HALF,) + tile, F32),
        pltpu.VMEM((HALF,) + tile, F32),
        pltpu.VMEM((2 * HALF,) + tile, F32),
        firsts,
        seconds,
        thirds,
        sums1,
        sums2,
    ]


def greet(place, barrier, devices):
    for device in devices:
        pl.semaphore_signal(barrier, inc=1, device_id=device, device_id_type=MESH)


def tiles_in(local, enc, rel):
    for column in range(4):
        half, low = column // 2 * HALF, column % 2
        tiles = enc[:, column * 128 : column * 128 + 128].reshape(96, 8, 128)
        local[half + low * 96 : half + low * 96 + 96] = tiles
        tiles = rel[:, column * 128 : column * 128 + 128].reshape(2, 8, 128)
        local[half + 192 + low * 2 : half + 194 + low * 2] = tiles


def tiles_out(full, enc_ref, rel_ref):
    g = lax.axis_index("rel")
    for column in range(4):
        half, low = column // 2 * HALF, column % 2
        lanes = pl.ds(column * 128, 128)
        enc_ref[:, lanes] = full[half + low * 96 : half + low * 96 + 96].reshape(768, 128)
        rows = full[half + 192 + low * 2 : half + 194 + low * 2].reshape(16, 128)
        part = jnp.zeros((3, 128), F32)
        for group in range(4):
            part = jnp.where(g == group, rows[group * 3 : group * 3 + 3], part)
        rel_ref[:, lanes] = part


NT = (((1,), (1,)), ((), ()))
ROWS = 768
AUG = 320


def dot(a, b, dims=(((1,), (0,)), ((), ()))):
    return lax.dot_general(a, b, dims, preferred_element_type=F32)


def two_terms(value):
    high = value.astype(BF16)
    return high, (value - high.astype(F32)).astype(BF16)


def is_row(count, width, ids):
    return lax.broadcasted_iota(jnp.int32, (count, width), 0) == ids


def one_hot(count, width, ids):
    return jnp.where(is_row(count, width, ids), 1.0, 0.0).astype(BF16)


def gather_edges(edge_src, edge_tgt, hot, neg, label, shift, edges, shifts):
    edges[...] = jnp.zeros(edges.shape, jnp.int32)
    for pair, slots in enumerate(((0, 1), (3, 2))):
        for s, slot in enumerate(slots):
            row = slice(slot, slot + 1)
            which = hot[0, 0, slot, 1:2, :] + 2 * hot[0, 0, slot, 2:3, :]
            edges[pair, 4 * s : 4 * s + 1, 0:ROWS] = edge_src[0, 0, row, :]
            edges[pair, 4 * s + 1 : 4 * s + 2, 0:ROWS] = which
            edges[pair, 4 * s + 2 : 4 * s + 3, 0:ROWS] = edge_tgt[0, 0, row, :]
            edges[pair, 4 * s + 3 : 4 * s + 4, 0:ROWS] = label[0, 0, row, :]
            edges[pair, 4 * s : 4 * s + 1, ROWS : ROWS + NEG] = neg[0, 0, row, :]
    shifts[...] = jnp.concatenate([shift[...].astype(F32), jnp.zeros((13, EMB), F32)], 0).astype(BF16)


def meet_pair(e, s, g, z_half, source_t, block, tgt_sum, mixed):
    scale = EMB ** (-0.5)
    src_ids, which = e[4 * s : 4 * s + 1, :ROWS], e[4 * s + 1 : 4 * s + 2, :ROWS]
    tgt_ids, label = e[4 * s + 2 : 4 * s + 3, :ROWS], e[4 * s + 3 : 4 * s + 4, :ROWS]
    neg_ids = e[4 * s : 4 * s + 1, ROWS : ROWS + NEG]
    ends = jnp.concatenate([one_hot(256, ROWS, src_ids), one_hot(64, ROWS, which + 16 * g)], 0)
    query = dot(source_t[...], ends).astype(BF16)
    rows = slice(256 * s, 256 * s + 256)
    prob = 1.0 / (1.0 + jnp.exp(-scale * dot(block[rows], query)))
    times = jnp.sum(
        jnp.where(is_row(256, NEG, neg_ids - 256 * z_half), 1.0, 0.0), axis=1, keepdims=True
    )
    weight = times * (prob * (1.0 / NEG)).astype(BF16).astype(F32)
    weight = weight + jnp.where(
        is_row(256, ROWS, tgt_ids - 256 * z_half), prob - label.astype(F32), 0.0
    )
    high, low = two_terms(weight)
    tgt_sum[rows] += dot(high, query, NT) + dot(low, query, NT)
    mixed[:, rows] += dot(ends, high, NT) + dot(ends, low, NT)


class Group:
    def __init__(self, place, send_sems, recv_sems):
        self.place, self.send_sems, self.recv_sems, self.used, self.open = place, send_sems, recv_sems, 0, []
        self.k, self.z_half = place.at["k"], lax.div(place.at["z"], 4)

    def device(self, dx, dy, dz, k):
        at = self.place.at
        return self.place.device(
            x=lax.rem(at["x"] + 2 * dx, 4),
            y=at["y"] + dy * (1 - 2 * lax.rem(at["y"], 2)),
            z=lax.rem(at["z"] + 4 * dz, 8),
            k=k,
        )

    def peers(self):
        found = [
            self.device(dx, 0, dz, k) for dx in range(2) for dz in range(2) for k in range(2) if dx + dz
        ]
        return found + [self.place.other_core(), self.device(0, 1, 0, 0), self.device(0, 1, 0, 1)]

    def copy(self, src, dst, device, sem):
        made = pltpu.make_async_remote_copy(
            src_ref=src,
            dst_ref=dst,
            send_sem=self.send_sems.at[self.used],
            recv_sem=self.recv_sems.at[sem],
            device_id=device,
            device_id_type=MESH,
        )
        self.used += 1
        return made

    def send(self, src, dst, device, sem):
        made = self.copy(src, dst, device, sem)
        made.start()
        self.open.append((made, None))

    def send_if(self, when, src, dst, device, sem):
        made = self.copy(src, dst, device, sem)

        @pl.when(when)
        def _():
            made.start()

        self.open.append((made, when))

    def wait(self, dst, sem):
        pltpu.make_async_remote_copy(
            src_ref=dst,
            dst_ref=dst,
            send_sem=self.send_sems.at[0],
            recv_sem=self.recv_sems.at[sem],
            device_id=self.place.other_core(),
            device_id_type=MESH,
        ).wait_recv()

    def wait_if(self, when, dst, sem):
        @pl.when(when)
        def _():
            self.wait(dst, sem)

    def finish(self):
        for made, when in self.open:
            if when is None:
                made.wait_send()
            else:
                pl.when(when)(made.wait_send)


RECVS = 4 + 4 + 4 + 4 + 4 + 4
SENDS = 4 + 4 + 4 + 3 + 4 + 3


def meets(
    place, group, src_feat, tgt_feat, weight, shift, edge_src, edge_tgt, hot, neg, label, src_grad,
    tgt_grad, edges, shifts, edges_in, source, source_t, block, own_rows, act, feat_t, tgt_sum, mixed,
    src_part, src_in, tgt_in, greeted,
):
    k, z_half, q = group.k, group.z_half, lax.axis_index("rel")
    scale = EMB ** (-0.5)
    gather_edges(edge_src, edge_tgt, hot, neg, label, shift, edges, shifts)

    greeted()

    def to_consumers(kind, src_of, dst):
        for dx in range(2):
            for dz in range(2):
                args = (src_of(dx), dst, group.device(dx, 0, dz, dx), 4 * kind + 2 * dz + k)
                if dx + dz == 0:
                    group.send_if(k == 1, *args)
                else:
                    group.send(*args)

    shift_rows = pl.ds(256 + 16 * q, 16)
    to_consumers(0, lambda dx: edges.at[dx], edges_in.at[q])
    to_consumers(1, lambda dx: shifts, source.at[shift_rows])

    feats = jnp.concatenate([src_feat[...], tgt_feat[...]], 0)
    act[...] = jnp.tanh(dot(feats, weight[...]))
    own_rows[...] = act[...].astype(BF16)
    src_rows = pl.ds(64 * q, 64)
    to_consumers(2, lambda dx: own_rows.at[0:64], source.at[src_rows])
    for dy, there in ((0, 1 - k), (1, 0), (1, 1)):
        group.send(
            own_rows.at[64:192], block.at[pl.ds(256 * dy + 128 * k, 128)], group.device(0, dy, 0, there), 12 + 2 * dy + k
        )
    block[pl.ds(128 * k, 128)] = own_rows[64:192]

    @pl.when(k == 0)
    def _():
        edges_in[q] = edges[0]
        source[shift_rows] = shifts[...]
        source[src_rows] = own_rows[0:64]

    feat_t[...] = feats.astype(F32).T.astype(BF16)
    tgt_sum[...] = jnp.zeros(tgt_sum.shape, F32)
    mixed[...] = jnp.zeros(mixed.shape, F32)

    def from_producers(kind, dst_of):
        for dz in range(2):
            for there in range(2):
                theirs = lax.rem(z_half + dz, 2) * 2 + there
                args = (dst_of(theirs), 4 * kind + 2 * dz + there)
                if dz + there == 0:
                    group.wait_if(k == 1, *args)
                else:
                    group.wait(*args)

    from_producers(0, lambda g: edges_in.at[g])
    from_producers(1, lambda g: source.at[pl.ds(256 + 16 * g, 16)])
    from_producers(2, lambda g: source.at[pl.ds(64 * g, 64)])
    source_t[...] = source[...].astype(F32).T.astype(BF16)
    for dy, there in ((0, 1 - k), (1, 0), (1, 1)):
        group.wait(block.at[pl.ds(256 * dy + 128 * there, 128)], 12 + 2 * dy + there)

    @pl.loop(0, 4)
    def _(g):
        e = edges_in[g]
        for s in range(2):
            meet_pair(e, s, g, z_half, source_t, block, tgt_sum, mixed)

    high, low = two_terms(mixed[...])
    rows = block[...]
    src_part[...] = scale * (dot(high, rows) + dot(low, rows))
    for dz in range(2):
        for there in range(2):
            theirs = lax.rem(z_half + dz, 2) * 2 + there
            device = group.place.device(
                x=lax.rem(place.at["x"] + 2 * k, 4), z=lax.rem(place.at["z"] + 4 * dz, 8), k=there
            )
            args = (src_part.at[pl.ds(64 * theirs, 64)], src_in.at[2 * k + dz], device, 16 + 2 * k + dz)
            if dz + there == 0:
                group.send_if(k == 1, *args)
            else:
                group.send(*args)

    @pl.when(k == 0)
    def _():
        src_in[0] = src_part[pl.ds(64 * q, 64)]

    tgt_sum[...] = scale * tgt_sum[...]
    for dy, there in ((0, 1 - k), (1, 0), (1, 1)):
        group.send(
            tgt_sum.at[pl.ds(256 * dy + 128 * there, 128)], tgt_in.at[2 * dy + k], group.device(0, dy, 0, there), 20 + 2 * dy + k
        )
    group.wait_if(k == 1, src_in.at[0], 16)
    for slot in range(1, 4):
        group.wait(src_in.at[slot], 16 + slot)
    total = src_in[0] + src_in[1] + src_in[2] + src_in[3]
    src_grad[...] = total
    d_src = (total * (1.0 - act[0:64] * act[0:64])).astype(BF16)
    total = tgt_sum[pl.ds(128 * k, 128)]
    for dy, there in ((0, 1 - k), (1, 0), (1, 1)):
        group.wait(tgt_in.at[2 * dy + there], 20 + 2 * dy + there)
        total = total + tgt_in[2 * dy + there]
    tgt_grad[...] = total
    d_tgt = (total * (1.0 - act[64:192] * act[64:192])).astype(BF16)
    enc = dot(feat_t[...], jnp.concatenate([d_src, d_tgt], 0))
    rel = jnp.concatenate([src_part[256 + 16 * g : 259 + 16 * g] for g in range(4)] + [jnp.zeros((4, EMB), F32)], 0)
    return enc, rel


def scratch_of_meets():
    return [
        pltpu.VMEM((2, 8, 896), jnp.int32),
        pltpu.VMEM((16, EMB), BF16),
        pltpu.VMEM((4, 8, 896), jnp.int32),
        pltpu.VMEM((AUG, EMB), BF16),
        pltpu.VMEM((EMB, AUG), BF16),
        pltpu.VMEM((512, EMB), BF16),
        pltpu.VMEM((192, EMB), BF16),
        pltpu.VMEM((192, EMB), F32),
        pltpu.VMEM((768, 192), BF16),
        pltpu.VMEM((512, EMB), F32),
        pltpu.VMEM((AUG, 512), F32),
        pltpu.VMEM((AUG, EMB), F32),
        pltpu.VMEM((4, 64, EMB), F32),
        pltpu.VMEM((4, 128, EMB), F32),
    ]

def reduce_kernel(enc_ref, rel_ref, enc_out, rel_out, *scratch):
    *buffers, send_sems, recv_sems = scratch
    place = Place()
    barrier = pltpu.get_barrier_semaphore()
    others = [place.along(axis, apart)[1] for axis, n in AXIS.items() for apart in range(1, n)]
    others.append(place.other_core())
    greet(place, barrier, others)
    tiles_in(buffers[0], enc_ref[...], rel_ref[...])
    pl.semaphore_wait(barrier, len(others))
    wires = Wires(send_sems, recv_sems)
    reduce_everywhere(place, wires, *buffers)
    tiles_out(buffers[3], enc_out, rel_out)
    wires.finish()

def summed(enc, rel):
    return pl.pallas_call(
        reduce_kernel,
        out_shape=(jax.ShapeDtypeStruct((768, EMB), F32), jax.ShapeDtypeStruct((3, EMB), F32)),
        in_specs=[pl.BlockSpec(memory_space=pltpu.VMEM)] * 2,
        out_specs=(pl.BlockSpec(memory_space=pltpu.VMEM),) * 2,
        scratch_shapes=scratch_of_reduce()
        + [pltpu.SemaphoreType.DMA((WIRES,)), pltpu.SemaphoreType.DMA((WIRES,))],
        compiler_params=pltpu.CompilerParams(
            collective_id=0, has_side_effects=True, vmem_limit_bytes=40 * 2**20
        ),
    )(enc, rel)


def meet_kernel(*refs):
    inputs, (src_grad, tgt_grad, enc, rel), scratch = refs[:9], refs[9:13], refs[13:]
    *buffers, send_sems, recv_sems = scratch
    place = Place()
    group = Group(place, send_sems, recv_sems)
    barrier = pltpu.get_barrier_semaphore()
    others = group.peers()
    greet(place, barrier, others)
    enc[...], rel[...] = meets(
        place, group, *inputs, src_grad, tgt_grad, *buffers, lambda: pl.semaphore_wait(barrier, len(others))
    )
    group.finish()


def met(*arrays):
    shapes = ((64, EMB), (128, EMB), (768, EMB), (16, EMB))
    return pl.pallas_call(
        meet_kernel,
        out_shape=tuple(jax.ShapeDtypeStruct(shape, F32) for shape in shapes),
        in_specs=[pl.BlockSpec(memory_space=pltpu.VMEM)] * 9,
        out_specs=(pl.BlockSpec(memory_space=pltpu.VMEM),) * 4,
        scratch_shapes=scratch_of_meets()
        + [pltpu.SemaphoreType.DMA((SENDS,)), pltpu.SemaphoreType.DMA((RECVS,))],
        compiler_params=pltpu.CompilerParams(
            collective_id=1, has_side_effects=True, vmem_limit_bytes=48 * 2**20
        ),
    )(*arrays)


def shards(*arrays):
    src_grad, tgt_grad, enc, rel = met(*arrays)
    enc_grad, rel_grad = summed(enc, rel)
    return src_grad, tgt_grad, rel_grad, enc_grad


def solution(mesh):
    in_specs = (
        P(("bucket", "rel"), None),
        P(("bucket", "rel"), None),
        P(),
        P("rel", None),
        P("bucket", "rel", None, None),
        P("bucket", "rel", None, None),
        P("bucket", "rel", None, None, None),
        P("bucket", "rel", None, None),
        P("bucket", "rel", None, None),
    )
    out_specs = (P(("bucket", "rel"), None), P(("bucket", "rel"), None), P("rel", None), P())
    return jax.shard_map(shards, mesh=mesh, in_specs=in_specs, out_specs=out_specs, check_vma=False)
```

```python
import jax
import jax.numpy as jnp
from jax import lax
from jax.experimental import pallas as pl
from jax.experimental.pallas import tpu as pltpu
from jax.sharding import PartitionSpec as P

EMB = 512
NEG = 128
MEETS = 4
F32 = jnp.float32
BF16 = jnp.bfloat16
MESH = pl.DeviceIdType.MESH
AXIS = {"x": 4, "y": 8, "z": 8}
HALF = 224
PARTS = (("z", "y", "x", 0, 64), ("y", "z", "x", 64, 64), ("x", "y", "z", 128, 96))


def far_first(axis):
    n = AXIS[axis]
    return sorted(range(1, n), key=lambda apart: -min(apart, n - apart))


class Place:
    def __init__(self):
        b, q = lax.axis_index("bucket"), lax.axis_index("rel")
        self.at = {
            "x": lax.div(b, 32),
            "y": lax.rem(b, 8),
            "z": lax.div(q, 2) * 4 + lax.rem(lax.div(b, 8), 4),
            "k": lax.rem(q, 2),
        }

    def device(self, **moved):
        at = dict(self.at, **moved)
        bucket = at["x"] * 32 + lax.rem(at["z"], 4) * 8 + at["y"]
        return bucket, lax.div(at["z"], 4) * 2 + at["k"]

    def along(self, axis, apart):
        there = lax.rem(self.at[axis] + apart, AXIS[axis])
        return there, self.device(**{axis: there})

    def other_core(self):
        return self.device(k=1 - self.at["k"])


class Wires:
    def __init__(self, send_sems, recv_sems):
        self.send_sems, self.recv_sems, self.used, self.open = send_sems, recv_sems, 0, []

    def send(self, src, dst, device):
        copy = pltpu.make_async_remote_copy(
            src_ref=src,
            dst_ref=dst,
            send_sem=self.send_sems.at[self.used],
            recv_sem=self.recv_sems.at[self.used],
            device_id=device,
            device_id_type=MESH,
        )
        copy.start()
        self.used += 1
        self.open.append(copy)
        return copy

    def finish(self):
        for copy in self.open:
            copy.wait_send()


def reduce_everywhere(place, wires, local, pair, mine, full, firsts, seconds, thirds, sums1, sums2, fill):
    at, k = place.at, place.at["k"]
    other = place.other_core()
    copies = []
    fill(1 - k)
    for _, _, _, base, size in PARTS:
        size = min(size, 196 - base)
        copies.append(
            wires.send(local.at[pl.ds((1 - k) * HALF + base, size)], pair.at[pl.ds(base, size)], other)
        )
    fill(k)
    mine[pl.ds(196, 28)] = jnp.zeros((28, 8, 128), F32)
    pending1 = []
    for p, (first, _, _, base, size) in enumerate(PARTS):
        copies[p].wait_recv()
        real = min(size, 196 - base)
        mine[pl.ds(base, real)] = local[pl.ds(k * HALF + base, real)] + pair[pl.ds(base, real)]
        block = size // AXIS[first]
        here = {}
        for apart in far_first(first):
            there, device = place.along(first, apart)
            here[apart] = wires.send(mine.at[pl.ds(base + there * block, block)], firsts[p].at[apart], device)
        pending1.append(here)
    pending2 = []
    for p, (first, second, _, base, size) in enumerate(PARTS):
        block = size // AXIS[first]
        total = mine[pl.ds(base + at[first] * block, block)]
        for apart in range(1, AXIS[first]):
            pending1[p][apart].wait_recv()
            total = total + firsts[p][apart]
        sums1[p][...] = total
        small = block // AXIS[second]
        here = {}
        for apart in far_first(second):
            there, device = place.along(second, apart)
            here[apart] = wires.send(sums1[p].at[pl.ds(there * small, small)], seconds[p].at[apart], device)
        pending2.append(here)
    pending3 = []
    for p, (first, second, third, base, size) in enumerate(PARTS):
        small = size // AXIS[first] // AXIS[second]
        total = sums1[p][pl.ds(at[second] * small, small)]
        for apart in range(1, AXIS[second]):
            pending2[p][apart].wait_recv()
            total = total + seconds[p][apart]
        sums2[p][...] = total
        here = {}
        for apart in far_first(third):
            here[apart] = wires.send(sums2[p], thirds[p].at[apart], place.along(third, apart)[1])
        pending3.append(here)
    pending4 = []
    for p, (first, second, third, base, size) in enumerate(PARTS):
        thirds[p][0] = sums2[p][...]
        for apart in range(1, AXIS[third]):
            pending3[p][apart].wait_recv()
        total = 0.0
        for where in range(AXIS[third]):
            total = total + thirds[p][lax.rem(at[third] + AXIS[third] - where, AXIS[third])]
        block = size // AXIS[first]
        small = block // AXIS[second]
        own = k * HALF + base + at[first] * block + at[second] * small
        full[pl.ds(own, small)] = total
        here = []
        for apart in far_first(second):
            piece = full.at[pl.ds(own, small)]
            here.append(wires.send(piece, piece, place.along(second, apart)[1]))
        pending4.append(here)
    pending5, pending6 = [], []
    for p, (first, second, third, base, size) in enumerate(PARTS):
        block = size // AXIS[first]
        for copy in pending4[p]:
            copy.wait_recv()
        piece = full.at[pl.ds(k * HALF + base + at[first] * block, block)]
        pending5.append(
            {apart: wires.send(piece, piece, place.along(first, apart)[1]) for apart in far_first(first)}
        )
        pending6.append(wires.send(piece, piece, other))
    for p, (first, second, third, base, size) in enumerate(PARTS):
        block = size // AXIS[first]
        for apart in reversed(far_first(first)):
            pending5[p][apart].wait_recv()
            start = lax.rem(at[first] + AXIS[first] - apart, AXIS[first])
            piece = full.at[pl.ds(k * HALF + base + start * block, block)]
            pending6.append(wires.send(piece, piece, other))
    for copy in pending6:
        copy.wait_recv()


WIRES = 3 + 17 + 21 + 13 + 21 + 17 + 20


def scratch_of_reduce():
    tile = (8, 128)
    firsts = [pltpu.VMEM((AXIS[f], n // AXIS[f]) + tile, F32) for f, s, t, _, n in PARTS]
    small = [n // AXIS[f] // AXIS[s] for f, s, t, _, n in PARTS]
    seconds = [pltpu.VMEM((AXIS[p[1]], m) + tile, F32) for p, m in zip(PARTS, small)]
    thirds = [pltpu.VMEM((AXIS[p[2]], m) + tile, F32) for p, m in zip(PARTS, small)]
    sums1 = [pltpu.VMEM((n // AXIS[f],) + tile, F32) for f, s, t, _, n in PARTS]
    sums2 = [pltpu.VMEM((m,) + tile, F32) for m in small]
    return [
        pltpu.VMEM((2 * HALF,) + tile, F32),
        pltpu.VMEM((HALF,) + tile, F32),
        pltpu.VMEM((HALF,) + tile, F32),
        pltpu.VMEM((2 * HALF,) + tile, F32),
        firsts,
        seconds,
        thirds,
        sums1,
        sums2,
    ]


def greet(place, barrier, devices):
    for device in devices:
        pl.semaphore_signal(barrier, inc=1, device_id=device, device_id_type=MESH)


def tiles_out(full, enc_ref, rel_ref):
    g = lax.axis_index("rel")
    for column in range(4):
        half, low = column // 2 * HALF, column % 2
        lanes = pl.ds(column * 128, 128)
        enc_ref[:, lanes] = full[half + low * 96 : half + low * 96 + 96].reshape(768, 128)
        rows = full[half + 192 + low * 2 : half + 194 + low * 2].reshape(16, 128)
        part = jnp.zeros((3, 128), F32)
        for group in range(4):
            part = jnp.where(g == group, rows[group * 3 : group * 3 + 3], part)
        rel_ref[:, lanes] = part


NT = (((1,), (1,)), ((), ()))
ROWS = 768
AUG = 320


def dot(a, b, dims=(((1,), (0,)), ((), ()))):
    return lax.dot_general(a, b, dims, preferred_element_type=F32)


def two_terms(value):
    high = value.astype(BF16)
    return high, (value - high.astype(F32)).astype(BF16)


def is_row(count, width, ids):
    return lax.broadcasted_iota(jnp.int32, (count, width), 0) == ids


def one_hot(count, width, ids):
    return jnp.where(is_row(count, width, ids), 1.0, 0.0).astype(BF16)


def gather_edges(edge_src, edge_tgt, hot, neg, label, shift, edges, shifts):
    edges[...] = jnp.zeros(edges.shape, jnp.int16)
    for pair, slots in enumerate(((0, 1), (3, 2))):
        for s, slot in enumerate(slots):
            row = slice(slot, slot + 1)
            whole = [
                edge_src[0, 0, row, :],
                edge_tgt[0, 0, row, :],
                label[0, 0, row, :],
                hot[0, 0, 1, row, :],
                hot[0, 0, 2, row, :],
            ]
            rows = [part[:, h : h + ROWS // 2] for part in whole for h in (0, ROWS // 2)]
            rows.append(jnp.concatenate([neg[0, 0, row, :], jnp.zeros((1, ROWS // 2 - NEG), jnp.int32)], 1))
            rows.append(jnp.zeros((5, ROWS // 2), jnp.int32))
            edges[pair, 16 * s : 16 * s + 16] = jnp.concatenate(rows, 0).astype(jnp.int16)
    parts = [shift[:, c : c + 128].astype(F32) for c in range(0, EMB, 128)]
    shifts[...] = jnp.concatenate(parts + [jnp.zeros((4, 128), F32)], 0).astype(BF16)


def spread_shifts(shifts, source):
    for g in range(4):
        got = shifts[g].astype(F32)
        rows = jnp.concatenate([got[3 * c : 3 * c + 3] for c in range(4)], 1)
        source[256 + 16 * g : 272 + 16 * g] = jnp.concatenate([rows, jnp.zeros((13, EMB), F32)], 0).astype(BF16)


def meet_pair(e, s, g, z_half, source_t, block, tgt_sum, mixed):
    scale = EMB ** (-0.5)
    rows = [jnp.concatenate([e[i : i + 1], e[i + 1 : i + 2]], 1) for i in range(0, 10, 2)]
    src_ids, tgt_ids, label, which = rows[0], rows[1], rows[2], rows[3] + 2 * rows[4]
    neg_ids = e[10:11, :NEG]
    ends = jnp.concatenate([one_hot(256, ROWS, src_ids), one_hot(64, ROWS, which + 16 * g)], 0)
    query = dot(source_t[...], ends).astype(BF16)
    rows = slice(256 * s, 256 * s + 256)
    prob = 1.0 / (1.0 + jnp.exp(-scale * dot(block[rows], query)))
    times = jnp.sum(
        jnp.where(is_row(256, NEG, neg_ids - 256 * z_half), 1.0, 0.0), axis=1, keepdims=True
    )
    weight = times * (prob * (1.0 / NEG)).astype(BF16).astype(F32)
    weight = weight + jnp.where(
        is_row(256, ROWS, tgt_ids - 256 * z_half), prob - label.astype(F32), 0.0
    )
    high, low = two_terms(weight)
    tgt_sum[rows] += dot(high, query, NT) + dot(low, query, NT)
    mixed[:, rows] += dot(ends, high, NT) + dot(ends, low, NT)


class Group:
    def __init__(self, place, send_sems, recv_sems):
        self.place, self.send_sems, self.recv_sems, self.used, self.open = place, send_sems, recv_sems, 0, []
        self.k, self.z_half = place.at["k"], lax.div(place.at["z"], 4)

    def device(self, dx, dy, dz, k):
        at = self.place.at
        return self.place.device(
            x=lax.rem(at["x"] + 2 * dx, 4),
            y=at["y"] + dy * (1 - 2 * lax.rem(at["y"], 2)),
            z=lax.rem(at["z"] + 4 * dz, 8),
            k=k,
        )

    def peers(self):
        found = [self.device(dx, 0, dz, 1 - self.k) for dx, dz in ((0, 1), (1, 0), (1, 1))]
        return found + [self.device(1, 0, 1, self.k), self.device(0, 1, 0, 1 - self.k)]

    def copy(self, src, dst, device, sem):
        made = pltpu.make_async_remote_copy(
            src_ref=src,
            dst_ref=dst,
            send_sem=self.send_sems.at[self.used],
            recv_sem=self.recv_sems.at[sem],
            device_id=device,
            device_id_type=MESH,
        )
        self.used += 1
        return made

    def send(self, src, dst, device, sem):
        made = self.copy(src, dst, device, sem)
        made.start()
        self.open.append((made, None))

    def send_if(self, when, src, dst, device, sem):
        made = self.copy(src, dst, device, sem)

        @pl.when(when)
        def _():
            made.start()

        self.open.append((made, when))

    def wait(self, dst, sem):
        pltpu.make_async_remote_copy(
            src_ref=dst,
            dst_ref=dst,
            send_sem=self.send_sems.at[0],
            recv_sem=self.recv_sems.at[sem],
            device_id=self.place.other_core(),
            device_id_type=MESH,
        ).wait_recv()

    def wait_if(self, when, dst, sem):
        @pl.when(when)
        def _():
            self.wait(dst, sem)

    def finish(self):
        for made, when in self.open:
            if when is None:
                made.wait_send()
            else:
                pl.when(when)(made.wait_send)


RECVS = 4 + 4 + 4 + 4 + 4 + 4
SENDS = 4 + 4 + 4 + 3 + 4 + 3


def meets(
    place, group, fetched, edges, shifts, edges_in, shifts_in, source, source_t, block, own_rows, act,
    feat_t, tgt_sum, mixed, src_part, src_in, tgt_in, grads, src_grad, tgt_grad, greeted,
):
    k, z_half, q = group.k, group.z_half, lax.axis_index("rel")
    scale = EMB ** (-0.5)
    src_feat, tgt_feat, weight, shift, edge_src, edge_tgt, hot, neg, label = fetched
    for ref in (edge_src, edge_tgt, hot, neg, label, shift):
        ref.wait()
    gather_edges(*(ref.here for ref in (edge_src, edge_tgt, hot, neg, label, shift)), edges, shifts)
    for ref in (src_feat, tgt_feat, weight):
        ref.wait()
    feats = jnp.concatenate([src_feat.here[...], tgt_feat.here[...]], 0)
    act[...] = jnp.tanh(dot(feats, weight.here[...]))
    own_rows[...] = act[...].astype(BF16)

    greeted()

    def to_consumers(kind, src_of, dst):
        for dx in range(2):
            for dz in (1, 0):
                args = (src_of(dx), dst, group.device(dx, 0, dz, dx), 4 * kind + 2 * dz + k)
                if dx + dz == 0:
                    group.send_if(k == 1, *args)
                else:
                    group.send(*args)

    src_rows = pl.ds(64 * q, 64)
    to_consumers(2, lambda dx: own_rows.at[0:64], source.at[src_rows])
    to_consumers(0, lambda dx: edges.at[dx], edges_in.at[q])
    to_consumers(1, lambda dx: shifts, shifts_in.at[q])
    for dy, there in ((1, 0), (1, 1), (0, 1 - k)):
        group.send(
            own_rows.at[64:192], block.at[pl.ds(256 * dy + 128 * k, 128)], group.device(0, dy, 0, there), 12 + 2 * dy + k
        )
    block[pl.ds(128 * k, 128)] = own_rows[64:192]

    @pl.when(k == 0)
    def _():
        edges_in[q] = edges[0]
        shifts_in[q] = shifts[...]
        source[src_rows] = own_rows[0:64]

    feat_t[...] = feats.astype(F32).T.astype(BF16)
    tgt_sum[...] = jnp.zeros(tgt_sum.shape, F32)
    mixed[...] = jnp.zeros(mixed.shape, F32)

    def from_producers(kind, dst_of):
        for dz in range(2):
            for there in range(2):
                theirs = lax.rem(z_half + dz, 2) * 2 + there
                args = (dst_of(theirs), 4 * kind + 2 * dz + there)
                if dz + there == 0:
                    group.wait_if(k == 1, *args)
                else:
                    group.wait(*args)

    from_producers(0, lambda g: edges_in.at[g])
    from_producers(1, lambda g: shifts_in.at[g])
    spread_shifts(shifts_in, source)
    from_producers(2, lambda g: source.at[pl.ds(64 * g, 64)])
    source_t[...] = source[...].astype(F32).T.astype(BF16)
    for dy, there in ((0, 1 - k), (1, 0), (1, 1)):
        group.wait(block.at[pl.ds(256 * dy + 128 * there, 128)], 12 + 2 * dy + there)

    def send_tgt(dy, there):
        rows = pl.ds(256 * dy + 128 * there, 128)
        tgt_sum[rows] = scale * tgt_sum[rows]
        group.send(
            tgt_sum.at[rows], tgt_in.at[2 * dy + k], group.device(0, dy, 0, there), 20 + 2 * dy + k
        )

    for s in (1, 0):

        @pl.loop(0, 2)
        def _(turn):
            for g in range(2):
                e = edges_in[2 * turn + g, 16 * s : 16 * s + 16].astype(jnp.int32)
                meet_pair(e, s, 2 * turn + g, z_half, source_t, block, tgt_sum, mixed)

        if s == 1:
            send_tgt(1, 0)
            send_tgt(1, 1)

    high, low = two_terms(mixed[...])
    rows = block[...]
    src_part[...] = scale * (dot(high, rows) + dot(low, rows))
    for dz in (1, 0):
        for there in range(2):
            theirs = lax.rem(z_half + dz, 2) * 2 + there
            device = group.place.device(
                x=lax.rem(place.at["x"] + 2 * k, 4), z=lax.rem(place.at["z"] + 4 * dz, 8), k=there
            )
            args = (src_part.at[pl.ds(64 * theirs, 64)], src_in.at[2 * k + dz], device, 16 + 2 * k + dz)
            if dz + there == 0:
                group.send_if(k == 1, *args)
            else:
                group.send(*args)

    @pl.when(k == 0)
    def _():
        src_in[0] = src_part[pl.ds(64 * q, 64)]

    send_tgt(0, 1 - k)
    total = scale * tgt_sum[pl.ds(128 * k, 128)]
    for dy, there in ((0, 1 - k), (1, 0), (1, 1)):
        group.wait(tgt_in.at[2 * dy + there], 20 + 2 * dy + there)
        total = total + tgt_in[2 * dy + there]
    tgt_grad[...] = total
    grads[64:192] = (total * (1.0 - act[64:192] * act[64:192])).astype(BF16)
    group.wait_if(k == 1, src_in.at[0], 16)
    for slot in range(1, 4):
        group.wait(src_in.at[slot], 16 + slot)
    total = src_in[0] + src_in[1] + src_in[2] + src_in[3]
    src_grad[...] = total
    grads[0:64] = (total * (1.0 - act[0:64] * act[0:64])).astype(BF16)


def local_sums(half, local, feat_t, grads, src_part):
    lanes = pl.ds(pl.multiple_of(256 * half, 256), 256)
    enc = dot(feat_t[...], grads[:, lanes])
    rel = [src_part[256 + 16 * g : 259 + 16 * g, lanes] for g in range(4)]
    rel = jnp.concatenate(rel + [jnp.zeros((4, 256), F32)], 0)
    for low in range(2):
        cut = slice(128 * low, 128 * low + 128)
        local[pl.ds(half * HALF + low * 96, 96)] = enc[:, cut].reshape(96, 8, 128)
        local[pl.ds(half * HALF + 192 + low * 2, 2)] = rel[:, cut].reshape(2, 8, 128)


def scratch_of_meets():
    return [
        pltpu.VMEM((2, 32, 384), jnp.int16),
        pltpu.VMEM((16, 128), BF16),
        pltpu.VMEM((4, 32, 384), jnp.int16),
        pltpu.VMEM((4, 16, 128), BF16),
        pltpu.VMEM((AUG, EMB), BF16),
        pltpu.VMEM((EMB, AUG), BF16),
        pltpu.VMEM((512, EMB), BF16),
        pltpu.VMEM((192, EMB), BF16),
        pltpu.VMEM((192, EMB), F32),
        pltpu.VMEM((768, 192), BF16),
        pltpu.VMEM((512, EMB), F32),
        pltpu.VMEM((AUG, 512), F32),
        pltpu.VMEM((AUG, EMB), F32),
        pltpu.VMEM((4, 64, EMB), F32),
        pltpu.VMEM((4, 128, EMB), F32),
        pltpu.VMEM((192, EMB), BF16),
    ]


class Fetched:
    def __init__(self, there, here, sem):
        self.here, self.copy = here, pltpu.make_async_copy(there, here, sem)
        self.copy.start()

    def wait(self):
        self.copy.wait()


def kernel(*refs):
    inputs, outputs, (here, meet_buffers, sum_buffers, fetch_sems, *sems) = refs[:9], refs[9:13], refs[13:]
    src_grad, tgt_grad, enc_grad, rel_grad = outputs
    place = Place()
    group = Group(place, sems[0], sems[1])
    barrier = pltpu.get_barrier_semaphore()
    others = [place.along(axis, apart)[1] for axis, n in AXIS.items() for apart in range(1, n)]
    others += [place.other_core()] + group.peers()
    fetched = [None] * 9
    for i in (4, 5, 6, 7, 8, 3, 0, 1, 2):
        fetched[i] = Fetched(inputs[i], here[i], fetch_sems.at[i])
    greet(place, barrier, others)
    meets(
        place, group, fetched, *meet_buffers, src_grad, tgt_grad, lambda: pl.semaphore_wait(barrier, len(others))
    )
    feat_t, src_part, grads = meet_buffers[9], meet_buffers[12], meet_buffers[15]
    wires = Wires(sems[2], sems[3])
    reduce_everywhere(
        place, wires, *sum_buffers, lambda half: local_sums(half, sum_buffers[0], feat_t, grads, src_part)
    )
    tiles_out(sum_buffers[3], enc_grad, rel_grad)
    group.finish()
    wires.finish()


def hand_over(*refs):
    results, outputs, rooms, in_sems, out_sems = refs[:4], refs[4:8], *refs[8:]
    loads = [pltpu.make_async_copy(results[i], rooms[i], in_sems.at[i]) for i in range(4)]
    stores = [pltpu.make_async_copy(rooms[i], outputs[i], out_sems.at[i]) for i in range(4)]
    for load in loads:
        load.start()
    for load, store in zip(loads, stores):
        load.wait()
        store.start()
    for store in stores:
        store.wait()


def shards(*arrays):
    hot = jnp.transpose(arrays[6], (0, 1, 3, 2, 4))
    arrays = arrays[:6] + (hot,) + arrays[7:]
    shapes = ((64, EMB), (128, EMB), (768, EMB), (3, EMB))
    results = pl.pallas_call(
        kernel,
        out_shape=tuple(jax.ShapeDtypeStruct(shape, F32) for shape in shapes),
        in_specs=[pl.BlockSpec(memory_space=pl.ANY)] * 9,
        out_specs=(pl.BlockSpec(memory_space=pltpu.VMEM),) * 4,
        scratch_shapes=[
            [pltpu.VMEM(array.shape, array.dtype) for array in arrays],
            scratch_of_meets(),
            scratch_of_reduce(),
            pltpu.SemaphoreType.DMA((9,)),
            pltpu.SemaphoreType.DMA((SENDS,)),
            pltpu.SemaphoreType.DMA((RECVS,)),
            pltpu.SemaphoreType.DMA((WIRES,)),
            pltpu.SemaphoreType.DMA((WIRES,)),
        ],
        compiler_params=pltpu.CompilerParams(
            collective_id=0, has_side_effects=True, vmem_limit_bytes=56 * 2**20
        ),
    )(*arrays)
    src_grad, tgt_grad, enc_grad, rel_grad = pl.pallas_call(
        hand_over,
        out_shape=tuple(jax.ShapeDtypeStruct(shape, F32) for shape in shapes),
        in_specs=[pl.BlockSpec(memory_space=pl.ANY)] * 4,
        out_specs=(pl.BlockSpec(memory_space=pl.ANY),) * 4,
        scratch_shapes=[
            [pltpu.VMEM(shape, F32) for shape in shapes],
            pltpu.SemaphoreType.DMA((4,)),
            pltpu.SemaphoreType.DMA((4,)),
        ],
        compiler_params=pltpu.CompilerParams(vmem_limit_bytes=56 * 2**20),
    )(*results)
    return src_grad, tgt_grad, rel_grad, enc_grad


def solution(mesh):
    in_specs = (
        P(("bucket", "rel"), None),
        P(("bucket", "rel"), None),
        P(),
        P("rel", None),
        P("bucket", "rel", None, None),
        P("bucket", "rel", None, None),
        P("bucket", "rel", None, None, None),
        P("bucket", "rel", None, None),
        P("bucket", "rel", None, None),
    )
    out_specs = (P(("bucket", "rel"), None), P(("bucket", "rel"), None), P("rel", None), P())
    return jax.shard_map(shards, mesh=mesh, in_specs=in_specs, out_specs=out_specs, check_vma=False)
```

```python
import jax
import jax.numpy as jnp
from jax import lax
from jax.experimental import pallas as pl
from jax.experimental.pallas import tpu as pltpu
from jax.sharding import PartitionSpec as P

EMB = 512
NEG = 128
MEETS = 4
F32 = jnp.float32
BF16 = jnp.bfloat16
MESH = pl.DeviceIdType.MESH
AXIS = {"x": 4, "y": 8, "z": 8}
HALF = 224
PARTS = (("z", "y", "x", 0, 64), ("y", "z", "x", 64, 64), ("x", "y", "z", 128, 96))


def far_first(axis):
    n = AXIS[axis]
    return sorted(range(1, n), key=lambda apart: -min(apart, n - apart))


class Place:
    def __init__(self):
        b, q = lax.axis_index("bucket"), lax.axis_index("rel")
        self.at = {
            "x": lax.div(b, 32),
            "y": lax.rem(b, 8),
            "z": lax.div(q, 2) * 4 + lax.rem(lax.div(b, 8), 4),
            "k": lax.rem(q, 2),
        }

    def device(self, **moved):
        at = dict(self.at, **moved)
        bucket = at["x"] * 32 + lax.rem(at["z"], 4) * 8 + at["y"]
        return bucket, lax.div(at["z"], 4) * 2 + at["k"]

    def along(self, axis, apart):
        there = lax.rem(self.at[axis] + apart, AXIS[axis])
        return there, self.device(**{axis: there})

    def other_core(self):
        return self.device(k=1 - self.at["k"])


class Wires:
    def __init__(self, send_sems, recv_sems):
        self.send_sems, self.recv_sems, self.used, self.open = send_sems, recv_sems, 0, []

    def send(self, src, dst, device):
        copy = pltpu.make_async_remote_copy(
            src_ref=src,
            dst_ref=dst,
            send_sem=self.send_sems.at[self.used],
            recv_sem=self.recv_sems.at[self.used],
            device_id=device,
            device_id_type=MESH,
        )
        copy.start()
        self.used += 1
        self.open.append(copy)
        return copy

    def finish(self):
        for copy in self.open:
            copy.wait_send()


def reduce_everywhere(place, wires, local, pair, mine, full, firsts, seconds, thirds, sums1, sums2, fill):
    at, k = place.at, place.at["k"]
    other = place.other_core()
    copies = []
    fill(1 - k)
    for _, _, _, base, size in PARTS:
        size = min(size, 196 - base)
        copies.append(
            wires.send(local.at[pl.ds((1 - k) * HALF + base, size)], pair.at[pl.ds(base, size)], other)
        )
    fill(k)
    mine[pl.ds(196, 28)] = jnp.zeros((28, 8, 128), F32)
    pending1 = []
    for p, (first, _, _, base, size) in enumerate(PARTS):
        copies[p].wait_recv()
        real = min(size, 196 - base)
        mine[pl.ds(base, real)] = local[pl.ds(k * HALF + base, real)] + pair[pl.ds(base, real)]
        block = size // AXIS[first]
        here = {}
        for apart in far_first(first):
            there, device = place.along(first, apart)
            here[apart] = wires.send(mine.at[pl.ds(base + there * block, block)], firsts[p].at[apart], device)
        pending1.append(here)
    pending2 = []
    for p, (first, second, _, base, size) in enumerate(PARTS):
        block = size // AXIS[first]
        total = mine[pl.ds(base + at[first] * block, block)]
        for apart in range(1, AXIS[first]):
            pending1[p][apart].wait_recv()
            total = total + firsts[p][apart]
        sums1[p][...] = total
        small = block // AXIS[second]
        here = {}
        for apart in far_first(second):
            there, device = place.along(second, apart)
            here[apart] = wires.send(sums1[p].at[pl.ds(there * small, small)], seconds[p].at[apart], device)
        pending2.append(here)
    pending3 = []
    for p, (first, second, third, base, size) in enumerate(PARTS):
        small = size // AXIS[first] // AXIS[second]
        total = sums1[p][pl.ds(at[second] * small, small)]
        for apart in range(1, AXIS[second]):
            pending2[p][apart].wait_recv()
            total = total + seconds[p][apart]
        sums2[p][...] = total
        here = {}
        for apart in far_first(third):
            here[apart] = wires.send(sums2[p], thirds[p].at[apart], place.along(third, apart)[1])
        pending3.append(here)
    pending4 = []
    for p, (first, second, third, base, size) in enumerate(PARTS):
        thirds[p][0] = sums2[p][...]
        for apart in range(1, AXIS[third]):
            pending3[p][apart].wait_recv()
        total = 0.0
        for where in range(AXIS[third]):
            total = total + thirds[p][lax.rem(at[third] + AXIS[third] - where, AXIS[third])]
        block = size // AXIS[first]
        small = block // AXIS[second]
        own = k * HALF + base + at[first] * block + at[second] * small
        full[pl.ds(own, small)] = total
        here = []
        for apart in far_first(second):
            piece = full.at[pl.ds(own, small)]
            here.append(wires.send(piece, piece, place.along(second, apart)[1]))
        pending4.append(here)
    pending5, pending6 = [], []
    for p, (first, second, third, base, size) in enumerate(PARTS):
        block = size // AXIS[first]
        for copy in pending4[p]:
            copy.wait_recv()
        piece = full.at[pl.ds(k * HALF + base + at[first] * block, block)]
        pending5.append(
            {apart: wires.send(piece, piece, place.along(first, apart)[1]) for apart in far_first(first)}
        )
        pending6.append(wires.send(piece, piece, other))
    for p, (first, second, third, base, size) in enumerate(PARTS):
        block = size // AXIS[first]
        for apart in reversed(far_first(first)):
            pending5[p][apart].wait_recv()
            start = lax.rem(at[first] + AXIS[first] - apart, AXIS[first])
            piece = full.at[pl.ds(k * HALF + base + start * block, block)]
            pending6.append(wires.send(piece, piece, other))
    for copy in pending6:
        copy.wait_recv()


WIRES = 3 + 17 + 21 + 13 + 21 + 17 + 20


def scratch_of_reduce():
    tile = (8, 128)
    firsts = [pltpu.VMEM((AXIS[f], n // AXIS[f]) + tile, F32) for f, s, t, _, n in PARTS]
    small = [n // AXIS[f] // AXIS[s] for f, s, t, _, n in PARTS]
    seconds = [pltpu.VMEM((AXIS[p[1]], m) + tile, F32) for p, m in zip(PARTS, small)]
    thirds = [pltpu.VMEM((AXIS[p[2]], m) + tile, F32) for p, m in zip(PARTS, small)]
    sums1 = [pltpu.VMEM((n // AXIS[f],) + tile, F32) for f, s, t, _, n in PARTS]
    sums2 = [pltpu.VMEM((m,) + tile, F32) for m in small]
    return [
        pltpu.VMEM((2 * HALF,) + tile, F32),
        pltpu.VMEM((HALF,) + tile, F32),
        pltpu.VMEM((HALF,) + tile, F32),
        pltpu.VMEM((2 * HALF,) + tile, F32),
        firsts,
        seconds,
        thirds,
        sums1,
        sums2,
    ]


def greet(place, barrier, devices):
    for device in devices:
        pl.semaphore_signal(barrier, inc=1, device_id=device, device_id_type=MESH)


def tiles_out(full, enc_ref, rel_ref):
    g = lax.axis_index("rel")
    for column in range(4):
        half, low = column // 2 * HALF, column % 2
        lanes = pl.ds(column * 128, 128)
        enc_ref[:, lanes] = full[half + low * 96 : half + low * 96 + 96].reshape(768, 128)
        rows = full[half + 192 + low * 2 : half + 194 + low * 2].reshape(16, 128)
        part = jnp.zeros((3, 128), F32)
        for group in range(4):
            part = jnp.where(g == group, rows[group * 3 : group * 3 + 3], part)
        rel_ref[:, lanes] = part


NT = (((1,), (1,)), ((), ()))
ROWS = 768
AUG = 320


def dot(a, b, dims=(((1,), (0,)), ((), ()))):
    return lax.dot_general(a, b, dims, preferred_element_type=F32)


def two_terms(value):
    high = value.astype(BF16)
    return high, (value - high.astype(F32)).astype(BF16)


def is_row(count, width, ids):
    return lax.broadcasted_iota(jnp.int32, (count, width), 0) == ids


def one_hot(count, width, ids):
    return jnp.where(is_row(count, width, ids), 1.0, 0.0).astype(BF16)


def gather_edges(edge_src, edge_tgt, hot, neg, label, shift, edges, shifts):
    edges[...] = jnp.zeros(edges.shape, jnp.int16)
    for pair, slots in enumerate(((0, 1), (3, 2))):
        for s, slot in enumerate(slots):
            row = slice(slot, slot + 1)
            whole = [
                edge_src[0, 0, row, :],
                edge_tgt[0, 0, row, :],
                label[0, 0, row, :],
                hot[0, 0, 1, row, :],
                hot[0, 0, 2, row, :],
            ]
            rows = [part[:, h : h + ROWS // 2] for part in whole for h in (0, ROWS // 2)]
            rows.append(jnp.concatenate([neg[0, 0, row, :], jnp.zeros((1, ROWS // 2 - NEG), jnp.int32)], 1))
            rows.append(jnp.zeros((5, ROWS // 2), jnp.int32))
            edges[pair, 16 * s : 16 * s + 16] = jnp.concatenate(rows, 0).astype(jnp.int16)
    parts = [shift[:, c : c + 128].astype(F32) for c in range(0, EMB, 128)]
    shifts[...] = jnp.concatenate(parts + [jnp.zeros((4, 128), F32)], 0).astype(BF16)


def spread_shifts(shifts, source):
    for g in range(4):
        got = shifts[g].astype(F32)
        rows = jnp.concatenate([got[3 * c : 3 * c + 3] for c in range(4)], 1)
        source[256 + 16 * g : 272 + 16 * g] = jnp.concatenate([rows, jnp.zeros((13, EMB), F32)], 0).astype(BF16)


def meet_pair(e, s, g, z_half, source_t, block, tgt_sum, mixed):
    scale = EMB ** (-0.5)
    rows = [jnp.concatenate([e[i : i + 1], e[i + 1 : i + 2]], 1) for i in range(0, 10, 2)]
    src_ids, tgt_ids, label, which = rows[0], rows[1], rows[2], rows[3] + 2 * rows[4]
    neg_ids = e[10:11, :NEG]
    ends = jnp.concatenate([one_hot(256, ROWS, src_ids), one_hot(64, ROWS, which + 16 * g)], 0)
    query = dot(source_t[...], ends).astype(BF16)
    rows = slice(256 * s, 256 * s + 256)
    prob = 1.0 / (1.0 + jnp.exp(-scale * dot(block[rows], query)))
    times = jnp.sum(
        jnp.where(is_row(256, NEG, neg_ids - 256 * z_half), 1.0, 0.0), axis=1, keepdims=True
    )
    weight = times * (prob * (1.0 / NEG)).astype(BF16).astype(F32)
    weight = weight + jnp.where(
        is_row(256, ROWS, tgt_ids - 256 * z_half), prob - label.astype(F32), 0.0
    )
    high, low = two_terms(weight)
    tgt_sum[rows] += dot(high, query, NT) + dot(low, query, NT)
    mixed[:, rows] += dot(ends, high, NT) + dot(ends, low, NT)


def narrowed(value):
    most = jnp.maximum(jnp.max(jnp.abs(value), axis=0, keepdims=True), 1e-30)
    whole = jnp.floor(value * (32767.0 / most) + 0.5).astype(jnp.int32).astype(jnp.int16)
    step = most * (1.0 / 32767.0)
    rows = [step[:, c : c + 128] for c in range(0, EMB, 128)]
    return whole, jnp.concatenate(rows + [jnp.zeros((4, 128), F32)], 0)


def widened(whole, steps):
    step = jnp.concatenate([steps[c : c + 1] for c in range(4)], 1)
    return whole.astype(jnp.int32).astype(F32) * step


class Group:
    def __init__(self, place, send_sems, recv_sems):
        self.place, self.send_sems, self.recv_sems, self.used, self.open = place, send_sems, recv_sems, 0, []
        self.k, self.z_half = place.at["k"], lax.div(place.at["z"], 4)

    def device(self, dx, dy, dz, k):
        at = self.place.at
        return self.place.device(
            x=lax.rem(at["x"] + 2 * dx, 4),
            y=at["y"] + dy * (1 - 2 * lax.rem(at["y"], 2)),
            z=lax.rem(at["z"] + 4 * dz, 8),
            k=k,
        )

    def peers(self):
        found = [self.device(dx, 0, dz, 1 - self.k) for dx, dz in ((0, 1), (1, 0), (1, 1))]
        return found + [self.device(1, 0, 1, self.k), self.device(0, 1, 0, 1 - self.k)]

    def copy(self, src, dst, device, sem):
        made = pltpu.make_async_remote_copy(
            src_ref=src,
            dst_ref=dst,
            send_sem=self.send_sems.at[self.used],
            recv_sem=self.recv_sems.at[sem],
            device_id=device,
            device_id_type=MESH,
        )
        self.used += 1
        return made

    def send(self, src, dst, device, sem):
        made = self.copy(src, dst, device, sem)
        made.start()
        self.open.append((made, None))

    def send_if(self, when, src, dst, device, sem):
        made = self.copy(src, dst, device, sem)

        @pl.when(when)
        def _():
            made.start()

        self.open.append((made, when))

    def wait(self, dst, sem):
        pltpu.make_async_remote_copy(
            src_ref=dst,
            dst_ref=dst,
            send_sem=self.send_sems.at[0],
            recv_sem=self.recv_sems.at[sem],
            device_id=self.place.other_core(),
            device_id_type=MESH,
        ).wait_recv()

    def wait_if(self, when, dst, sem):
        @pl.when(when)
        def _():
            self.wait(dst, sem)

    def finish(self):
        for made, when in self.open:
            if when is None:
                made.wait_send()
            else:
                pl.when(when)(made.wait_send)


RECVS = 4 + 4 + 4 + 4 + 4 + 4 + 4
SENDS = 4 + 4 + 4 + 3 + 8 + 3


def meets(
    place, group, fetched, edges, shifts, edges_in, shifts_in, source, source_t, block, own_rows, act,
    feat_t, tgt_sum, mixed, src_part, src_in, tgt_in, grads, src_out, steps_out,
    steps_in, src_grad, tgt_grad, greeted,
):
    k, z_half, q = group.k, group.z_half, lax.axis_index("rel")
    scale = EMB ** (-0.5)
    src_feat, tgt_feat, weight, shift, edge_src, edge_tgt, hot, neg, label = fetched
    for ref in (edge_src, edge_tgt, hot, neg, label, shift):
        ref.wait()
    gather_edges(*(ref.here for ref in (edge_src, edge_tgt, hot, neg, label, shift)), edges, shifts)
    for ref in (src_feat, tgt_feat, weight):
        ref.wait()
    feats = jnp.concatenate([src_feat.here[...], tgt_feat.here[...]], 0)
    act[...] = jnp.tanh(dot(feats, weight.here[...]))
    own_rows[...] = act[...].astype(BF16)

    greeted()

    def to_consumers(kind, src_of, dst):
        for dx in range(2):
            for dz in (1, 0):
                args = (src_of(dx), dst, group.device(dx, 0, dz, dx), 4 * kind + 2 * dz + k)
                if dx + dz == 0:
                    group.send_if(k == 1, *args)
                else:
                    group.send(*args)

    src_rows = pl.ds(64 * q, 64)
    to_consumers(2, lambda dx: own_rows.at[0:64], source.at[src_rows])
    to_consumers(0, lambda dx: edges.at[dx], edges_in.at[q])
    to_consumers(1, lambda dx: shifts, shifts_in.at[q])
    for dy, there in ((1, 0), (1, 1), (0, 1 - k)):
        group.send(
            own_rows.at[64:192], block.at[pl.ds(256 * dy + 128 * k, 128)], group.device(0, dy, 0, there), 12 + 2 * dy + k
        )
    block[pl.ds(128 * k, 128)] = own_rows[64:192]

    @pl.when(k == 0)
    def _():
        edges_in[q] = edges[0]
        shifts_in[q] = shifts[...]
        source[src_rows] = own_rows[0:64]

    feat_t[...] = feats.astype(F32).T.astype(BF16)
    tgt_sum[...] = jnp.zeros(tgt_sum.shape, F32)
    mixed[...] = jnp.zeros(mixed.shape, F32)

    def from_producers(kind, dst_of):
        for dz in range(2):
            for there in range(2):
                theirs = lax.rem(z_half + dz, 2) * 2 + there
                args = (dst_of(theirs), 4 * kind + 2 * dz + there)
                if dz + there == 0:
                    group.wait_if(k == 1, *args)
                else:
                    group.wait(*args)

    from_producers(0, lambda g: edges_in.at[g])
    from_producers(1, lambda g: shifts_in.at[g])
    spread_shifts(shifts_in, source)
    from_producers(2, lambda g: source.at[pl.ds(64 * g, 64)])
    source_t[...] = source[...].astype(F32).T.astype(BF16)
    for dy, there in ((0, 1 - k), (1, 0), (1, 1)):
        group.wait(block.at[pl.ds(256 * dy + 128 * there, 128)], 12 + 2 * dy + there)

    def send_tgt(dy, there):
        rows = pl.ds(256 * dy + 128 * there, 128)
        tgt_sum[rows] = scale * tgt_sum[rows]
        group.send(
            tgt_sum.at[rows], tgt_in.at[2 * dy + k], group.device(0, dy, 0, there), 20 + 2 * dy + k
        )

    for s in (1, 0):

        @pl.loop(0, 2)
        def _(turn):
            for g in range(2):
                e = edges_in[2 * turn + g, 16 * s : 16 * s + 16].astype(jnp.int32)
                meet_pair(e, s, 2 * turn + g, z_half, source_t, block, tgt_sum, mixed)

        if s == 1:
            send_tgt(1, 0)
            send_tgt(1, 1)

    high, low = two_terms(mixed[...])
    rows = block[...]
    src_part[...] = scale * (dot(high, rows) + dot(low, rows))
    for part in range(4):
        rows = slice(64 * part, 64 * part + 64)
        src_out[rows], steps_out[part] = narrowed(src_part[rows])
    for dz in (1, 0):
        for there in range(2):
            theirs = lax.rem(z_half + dz, 2) * 2 + there
            device = group.place.device(
                x=lax.rem(place.at["x"] + 2 * k, 4), z=lax.rem(place.at["z"] + 4 * dz, 8), k=there
            )
            slot = 2 * k + dz
            both = (
                (src_out.at[pl.ds(64 * theirs, 64)], src_in.at[slot], device, 16 + slot),
                (steps_out.at[theirs], steps_in.at[slot], device, 24 + slot),
            )
            for args in both:
                if dz + there == 0:
                    group.send_if(k == 1, *args)
                else:
                    group.send(*args)

    @pl.when(k == 0)
    def _():
        src_in[0] = src_out[pl.ds(64 * q, 64)]
        steps_in[0] = steps_out[q]

    send_tgt(0, 1 - k)
    total = scale * tgt_sum[pl.ds(128 * k, 128)]
    for dy, there in ((0, 1 - k), (1, 0), (1, 1)):
        group.wait(tgt_in.at[2 * dy + there], 20 + 2 * dy + there)
        total = total + tgt_in[2 * dy + there]
    tgt_grad[...] = total
    grads[64:192] = (total * (1.0 - act[64:192] * act[64:192])).astype(BF16)
    group.wait_if(k == 1, src_in.at[0], 16)
    group.wait_if(k == 1, steps_in.at[0], 24)
    total = widened(src_in[0], steps_in[0])
    for slot in range(1, 4):
        group.wait(src_in.at[slot], 16 + slot)
        group.wait(steps_in.at[slot], 24 + slot)
        total = total + widened(src_in[slot], steps_in[slot])
    src_grad[...] = total
    grads[0:64] = (total * (1.0 - act[0:64] * act[0:64])).astype(BF16)


def local_sums(half, local, feat_t, grads, src_part):
    lanes = pl.ds(pl.multiple_of(256 * half, 256), 256)
    enc = dot(feat_t[...], grads[:, lanes])
    rel = [src_part[256 + 16 * g : 259 + 16 * g, lanes] for g in range(4)]
    rel = jnp.concatenate(rel + [jnp.zeros((4, 256), F32)], 0)
    for low in range(2):
        cut = slice(128 * low, 128 * low + 128)
        local[pl.ds(half * HALF + low * 96, 96)] = enc[:, cut].reshape(96, 8, 128)
        local[pl.ds(half * HALF + 192 + low * 2, 2)] = rel[:, cut].reshape(2, 8, 128)


def scratch_of_meets():
    return [
        pltpu.VMEM((2, 32, 384), jnp.int16),
        pltpu.VMEM((16, 128), BF16),
        pltpu.VMEM((4, 32, 384), jnp.int16),
        pltpu.VMEM((4, 16, 128), BF16),
        pltpu.VMEM((AUG, EMB), BF16),
        pltpu.VMEM((EMB, AUG), BF16),
        pltpu.VMEM((512, EMB), BF16),
        pltpu.VMEM((192, EMB), BF16),
        pltpu.VMEM((192, EMB), F32),
        pltpu.VMEM((768, 192), BF16),
        pltpu.VMEM((512, EMB), F32),
        pltpu.VMEM((AUG, 512), F32),
        pltpu.VMEM((AUG, EMB), F32),
        pltpu.VMEM((4, 64, EMB), jnp.int16),
        pltpu.VMEM((4, 128, EMB), F32),
        pltpu.VMEM((192, EMB), BF16),
        pltpu.VMEM((256, EMB), jnp.int16),
        pltpu.VMEM((4, 8, 128), F32),
        pltpu.VMEM((4, 8, 128), F32),
    ]


class Fetched:
    def __init__(self, there, here, sem):
        self.here, self.copy = here, pltpu.make_async_copy(there, here, sem)
        self.copy.start()

    def wait(self):
        self.copy.wait()


def kernel(*refs):
    inputs, outputs, (here, meet_buffers, sum_buffers, fetch_sems, *sems) = refs[:9], refs[9:13], refs[13:]
    src_grad, tgt_grad, enc_grad, rel_grad = outputs
    place = Place()
    group = Group(place, sems[0], sems[1])
    barrier = pltpu.get_barrier_semaphore()
    others = [place.along(axis, apart)[1] for axis, n in AXIS.items() for apart in range(1, n)]
    others += [place.other_core()] + group.peers()
    fetched = [None] * 9
    for i in (4, 5, 6, 7, 8, 3, 0, 1, 2):
        fetched[i] = Fetched(inputs[i], here[i], fetch_sems.at[i])
    greet(place, barrier, others)
    meets(
        place, group, fetched, *meet_buffers, src_grad, tgt_grad, lambda: pl.semaphore_wait(barrier, len(others))
    )
    feat_t, src_part, grads = meet_buffers[9], meet_buffers[12], meet_buffers[15]
    wires = Wires(sems[2], sems[3])
    reduce_everywhere(
        place, wires, *sum_buffers, lambda half: local_sums(half, sum_buffers[0], feat_t, grads, src_part)
    )
    tiles_out(sum_buffers[3], enc_grad, rel_grad)
    group.finish()
    wires.finish()


def hand_over(*refs):
    results, outputs, rooms, in_sems, out_sems = refs[:4], refs[4:8], *refs[8:]
    loads = [pltpu.make_async_copy(results[i], rooms[i], in_sems.at[i]) for i in range(4)]
    stores = [pltpu.make_async_copy(rooms[i], outputs[i], out_sems.at[i]) for i in range(4)]
    for load in loads:
        load.start()
    for load, store in zip(loads, stores):
        load.wait()
        store.start()
    for store in stores:
        store.wait()


def shards(*arrays):
    hot = jnp.transpose(arrays[6], (0, 1, 3, 2, 4))
    arrays = arrays[:6] + (hot,) + arrays[7:]
    shapes = ((64, EMB), (128, EMB), (768, EMB), (3, EMB))
    results = pl.pallas_call(
        kernel,
        out_shape=tuple(jax.ShapeDtypeStruct(shape, F32) for shape in shapes),
        in_specs=[pl.BlockSpec(memory_space=pl.ANY)] * 9,
        out_specs=(pl.BlockSpec(memory_space=pltpu.VMEM),) * 4,
        scratch_shapes=[
            [pltpu.VMEM(array.shape, array.dtype) for array in arrays],
            scratch_of_meets(),
            scratch_of_reduce(),
            pltpu.SemaphoreType.DMA((9,)),
            pltpu.SemaphoreType.DMA((SENDS,)),
            pltpu.SemaphoreType.DMA((RECVS,)),
            pltpu.SemaphoreType.DMA((WIRES,)),
            pltpu.SemaphoreType.DMA((WIRES,)),
        ],
        compiler_params=pltpu.CompilerParams(
            collective_id=0, has_side_effects=True, vmem_limit_bytes=56 * 2**20
        ),
    )(*arrays)
    src_grad, tgt_grad, enc_grad, rel_grad = pl.pallas_call(
        hand_over,
        out_shape=tuple(jax.ShapeDtypeStruct(shape, F32) for shape in shapes),
        in_specs=[pl.BlockSpec(memory_space=pl.ANY)] * 4,
        out_specs=(pl.BlockSpec(memory_space=pl.ANY),) * 4,
        scratch_shapes=[
            [pltpu.VMEM(shape, F32) for shape in shapes],
            pltpu.SemaphoreType.DMA((4,)),
            pltpu.SemaphoreType.DMA((4,)),
        ],
        compiler_params=pltpu.CompilerParams(vmem_limit_bytes=56 * 2**20),
    )(*results)
    return src_grad, tgt_grad, rel_grad, enc_grad


def solution(mesh):
    in_specs = (
        P(("bucket", "rel"), None),
        P(("bucket", "rel"), None),
        P(),
        P("rel", None),
        P("bucket", "rel", None, None),
        P("bucket", "rel", None, None),
        P("bucket", "rel", None, None, None),
        P("bucket", "rel", None, None),
        P("bucket", "rel", None, None),
    )
    out_specs = (P(("bucket", "rel"), None), P(("bucket", "rel"), None), P("rel", None), P())
    return jax.shard_map(shards, mesh=mesh, in_specs=in_specs, out_specs=out_specs, check_vma=False)
```

```python
import jax
import jax.numpy as jnp
from jax import lax
from jax.experimental import pallas as pl
from jax.experimental.pallas import tpu as pltpu
from jax.sharding import PartitionSpec as P

EMB = 512
NEG = 128
MEETS = 4
F32 = jnp.float32
BF16 = jnp.bfloat16
MESH = pl.DeviceIdType.MESH
AXIS = {"x": 4, "y": 8, "z": 8}
HALF = 224
PARTS = (("z", "y", "x", 0, 64), ("y", "z", "x", 64, 64), ("x", "y", "z", 128, 96))


def far_first(axis):
    n = AXIS[axis]
    return sorted(range(1, n), key=lambda apart: -min(apart, n - apart))


class Place:
    def __init__(self):
        b, q = lax.axis_index("bucket"), lax.axis_index("rel")
        self.at = {
            "x": lax.div(b, 32),
            "y": lax.rem(b, 8),
            "z": lax.div(q, 2) * 4 + lax.rem(lax.div(b, 8), 4),
            "k": lax.rem(q, 2),
        }

    def device(self, **moved):
        at = dict(self.at, **moved)
        bucket = at["x"] * 32 + lax.rem(at["z"], 4) * 8 + at["y"]
        return bucket, lax.div(at["z"], 4) * 2 + at["k"]

    def along(self, axis, apart):
        there = lax.rem(self.at[axis] + apart, AXIS[axis])
        return there, self.device(**{axis: there})

    def other_core(self):
        return self.device(k=1 - self.at["k"])


class Wires:
    def __init__(self, send_sems, recv_sems):
        self.send_sems, self.recv_sems, self.used, self.open = send_sems, recv_sems, 0, []

    def send(self, src, dst, device):
        copy = pltpu.make_async_remote_copy(
            src_ref=src,
            dst_ref=dst,
            send_sem=self.send_sems.at[self.used],
            recv_sem=self.recv_sems.at[self.used],
            device_id=device,
            device_id_type=MESH,
        )
        copy.start()
        self.used += 1
        self.open.append(copy)
        return copy

    def finish(self):
        for copy in self.open:
            copy.wait_send()


def packed(value):
    most = jnp.max(jnp.max(jnp.abs(value), axis=1, keepdims=True), axis=2, keepdims=True)
    power = jnp.ceil(jnp.log2(jnp.maximum(most, 1e-30)) - 14.99)
    whole = jnp.floor(value * jnp.exp2(-power) + 0.5)
    rows = jnp.broadcast_to(power, (value.shape[0], 1, 16, 128))
    return jnp.concatenate([whole, rows], 1).astype(jnp.int32).astype(jnp.int16)


def unpacked(blocks):
    wide = blocks.astype(jnp.int32).astype(F32)
    last = blocks.shape[1] - 1
    return wide[:, :last] * jnp.exp2(wide[:, last:])


def reduce_everywhere(place, wires, local, pair, mine, full, firsts, seconds, thirds, sums1, sums2, sent, gathered, final, fill):
    at, k = place.at, place.at["k"]
    other = place.other_core()
    copies = []
    for half in (0, HALF):
        local[half + 192 : half + 200] = jnp.zeros((8, 8, 128), F32)
    fill(1 - k)
    for _, _, _, base, size in PARTS:
        size = min(size, 204 - base)
        copies.append(
            wires.send(local.at[pl.ds((1 - k) * HALF + base, size)], pair.at[pl.ds(base, size)], other)
        )
    fill(k)
    mine[pl.ds(204, 20)] = jnp.zeros((20, 8, 128), F32)
    pending1 = []
    for p, (first, _, _, base, size) in enumerate(PARTS):
        copies[p].wait_recv()
        real = min(size, 204 - base)
        mine[pl.ds(base, real)] = local[pl.ds(k * HALF + base, real)] + pair[pl.ds(base, real)]
        block = size // AXIS[first]
        sent[p][...] = packed(mine[pl.ds(base, size)].reshape(AXIS[first], block // 2, 16, 128))
        here = {}
        for apart in far_first(first):
            there, device = place.along(first, apart)
            here[apart] = wires.send(sent[p].at[there], firsts[p].at[apart], device)
        pending1.append(here)
    pending2 = []
    for p, (first, second, _, base, size) in enumerate(PARTS):
        block = size // AXIS[first]
        total = mine[pl.ds(base + at[first] * block, block)]
        for apart in range(1, AXIS[first]):
            pending1[p][apart].wait_recv()
            total = total + unpacked(firsts[p][pl.ds(apart, 1)]).reshape(block, 8, 128)
        sums1[p][...] = total
        small = block // AXIS[second]
        here = {}
        for apart in far_first(second):
            there, device = place.along(second, apart)
            here[apart] = wires.send(sums1[p].at[pl.ds(there * small, small)], seconds[p].at[apart], device)
        pending2.append(here)
    pending3 = []
    for p, (first, second, third, base, size) in enumerate(PARTS):
        small = size // AXIS[first] // AXIS[second]
        total = sums1[p][pl.ds(at[second] * small, small)]
        for apart in range(1, AXIS[second]):
            pending2[p][apart].wait_recv()
            total = total + seconds[p][apart]
        sums2[p][...] = total
        here = {}
        for apart in far_first(third):
            here[apart] = wires.send(sums2[p], thirds[p].at[apart], place.along(third, apart)[1])
        pending3.append(here)
    pending4 = []
    for p, (first, second, third, base, size) in enumerate(PARTS):
        thirds[p][0] = sums2[p][...]
        for apart in range(1, AXIS[third]):
            pending3[p][apart].wait_recv()
        total = 0.0
        for where in range(AXIS[third]):
            total = total + thirds[p][lax.rem(at[third] + AXIS[third] - where, AXIS[third])]
        block = size // AXIS[first]
        small = block // AXIS[second]
        own = k * HALF + base + at[first] * block + at[second] * small
        full[pl.ds(own, small)] = total
        here = []
        for apart in far_first(second):
            piece = full.at[pl.ds(own, small)]
            here.append(wires.send(piece, piece, place.along(second, apart)[1]))
        pending4.append(here)
    pending5, pending6 = [], []
    for p, (first, second, third, base, size) in enumerate(PARTS):
        block = size // AXIS[first]
        for copy in pending4[p]:
            copy.wait_recv()
        own = full[pl.ds(k * HALF + base + at[first] * block, block)].reshape(1, block // 2, 16, 128)
        gathered[p][k, pl.ds(at[first], 1)] = packed(own)
        piece = gathered[p].at[k, at[first]]
        pending5.append(
            {apart: wires.send(piece, piece, place.along(first, apart)[1]) for apart in far_first(first)}
        )
    for p, (first, second, third, base, size) in enumerate(PARTS):
        for apart in reversed(far_first(first)):
            pending5[p][apart].wait_recv()
        piece = gathered[p].at[k]
        pending6.append(wires.send(piece, piece, other))
    for turn, half in enumerate((k, 1 - k)):
        for p, (first, second, third, base, size) in enumerate(PARTS):
            if turn:
                pending6[p].wait_recv()
            final[pl.ds(half * HALF + base, size)] = unpacked(gathered[p][half]).reshape(size, 8, 128)


WIRES = 3 + 17 + 21 + 13 + 21 + 17 + 3


def scratch_of_reduce():
    tile = (8, 128)
    coded = [(AXIS[f], n // AXIS[f] // 2 + 1, 16, 128) for f, s, t, _, n in PARTS]
    firsts = [pltpu.VMEM(shape, jnp.int16) for shape in coded]
    sent = [pltpu.VMEM(shape, jnp.int16) for shape in coded]
    gathered = [pltpu.VMEM((2,) + shape, jnp.int16) for shape in coded]
    small = [n // AXIS[f] // AXIS[s] for f, s, t, _, n in PARTS]
    seconds = [pltpu.VMEM((AXIS[p[1]], m) + tile, F32) for p, m in zip(PARTS, small)]
    thirds = [pltpu.VMEM((AXIS[p[2]], m) + tile, F32) for p, m in zip(PARTS, small)]
    sums1 = [pltpu.VMEM((n // AXIS[f],) + tile, F32) for f, s, t, _, n in PARTS]
    sums2 = [pltpu.VMEM((m,) + tile, F32) for m in small]
    return [
        pltpu.VMEM((2 * HALF,) + tile, F32),
        pltpu.VMEM((HALF,) + tile, F32),
        pltpu.VMEM((HALF,) + tile, F32),
        pltpu.VMEM((2 * HALF,) + tile, F32),
        firsts,
        seconds,
        thirds,
        sums1,
        sums2,
        sent,
        gathered,
        pltpu.VMEM((2 * HALF,) + tile, F32),
    ]


def greet(place, barrier, devices):
    for device in devices:
        pl.semaphore_signal(barrier, inc=1, device_id=device, device_id_type=MESH)


def tiles_out(full, enc_ref, rel_ref):
    g = lax.axis_index("rel")
    for column in range(4):
        half, low = column // 2 * HALF, column % 2
        lanes = pl.ds(column * 128, 128)
        enc_ref[:, lanes] = full[half + low * 96 : half + low * 96 + 96].reshape(768, 128)
        rows = full[half + 200 + low * 2 : half + 202 + low * 2].reshape(16, 128)
        part = jnp.zeros((3, 128), F32)
        for group in range(4):
            part = jnp.where(g == group, rows[group * 3 : group * 3 + 3], part)
        rel_ref[:, lanes] = part


NT = (((1,), (1,)), ((), ()))
ROWS = 768
AUG = 320


def dot(a, b, dims=(((1,), (0,)), ((), ()))):
    return lax.dot_general(a, b, dims, preferred_element_type=F32)


def two_terms(value):
    high = value.astype(BF16)
    return high, (value - high.astype(F32)).astype(BF16)


def is_row(count, width, ids):
    return lax.broadcasted_iota(jnp.int32, (count, width), 0) == ids


def one_hot(count, width, ids):
    return jnp.where(is_row(count, width, ids), 1.0, 0.0).astype(BF16)


def gather_edges(edge_src, edge_tgt, hot, neg, label, shift, edges, shifts):
    edges[...] = jnp.zeros(edges.shape, jnp.int16)
    for pair, slots in enumerate(((0, 1), (3, 2))):
        for s, slot in enumerate(slots):
            row = slice(slot, slot + 1)
            whole = [
                edge_src[0, 0, row, :],
                edge_tgt[0, 0, row, :],
                label[0, 0, row, :],
                hot[0, 0, 1, row, :],
                hot[0, 0, 2, row, :],
            ]
            rows = [part[:, h : h + ROWS // 2] for part in whole for h in (0, ROWS // 2)]
            rows.append(jnp.concatenate([neg[0, 0, row, :], jnp.zeros((1, ROWS // 2 - NEG), jnp.int32)], 1))
            rows.append(jnp.zeros((5, ROWS // 2), jnp.int32))
            edges[pair, 16 * s : 16 * s + 16] = jnp.concatenate(rows, 0).astype(jnp.int16)
    parts = [shift[:, c : c + 128].astype(F32) for c in range(0, EMB, 128)]
    shifts[...] = jnp.concatenate(parts + [jnp.zeros((4, 128), F32)], 0).astype(BF16)


def spread_shifts(shifts, source):
    for g in range(4):
        got = shifts[g].astype(F32)
        rows = jnp.concatenate([got[3 * c : 3 * c + 3] for c in range(4)], 1)
        source[256 + 16 * g : 272 + 16 * g] = jnp.concatenate([rows, jnp.zeros((13, EMB), F32)], 0).astype(BF16)


def meet_pair(e, s, g, z_half, source_t, block, tgt_sum, mixed):
    scale = EMB ** (-0.5)
    rows = [jnp.concatenate([e[i : i + 1], e[i + 1 : i + 2]], 1) for i in range(0, 10, 2)]
    src_ids, tgt_ids, label, which = rows[0], rows[1], rows[2], rows[3] + 2 * rows[4]
    neg_ids = e[10:11, :NEG]
    ends = jnp.concatenate([one_hot(256, ROWS, src_ids), one_hot(64, ROWS, which + 16 * g)], 0)
    query = dot(source_t[...], ends).astype(BF16)
    rows = slice(256 * s, 256 * s + 256)
    prob = 1.0 / (1.0 + jnp.exp(-scale * dot(block[rows], query)))
    times = jnp.sum(
        jnp.where(is_row(256, NEG, neg_ids - 256 * z_half), 1.0, 0.0), axis=1, keepdims=True
    )
    weight = times * (prob * (1.0 / NEG)).astype(BF16).astype(F32)
    weight = weight + jnp.where(
        is_row(256, ROWS, tgt_ids - 256 * z_half), prob - label.astype(F32), 0.0
    )
    high, low = two_terms(weight)
    tgt_sum[rows] += dot(high, query, NT) + dot(low, query, NT)
    mixed[:, rows] += dot(ends, high, NT) + dot(ends, low, NT)


def narrowed(value):
    most = jnp.maximum(jnp.max(jnp.abs(value), axis=0, keepdims=True), 1e-30)
    whole = jnp.floor(value * (32767.0 / most) + 0.5).astype(jnp.int32).astype(jnp.int16)
    step = most * (1.0 / 32767.0)
    rows = [step[:, c : c + 128] for c in range(0, EMB, 128)]
    return whole, jnp.concatenate(rows + [jnp.zeros((4, 128), F32)], 0)


def widened(whole, steps):
    step = jnp.concatenate([steps[c : c + 1] for c in range(4)], 1)
    return whole.astype(jnp.int32).astype(F32) * step


class Group:
    def __init__(self, place, send_sems, recv_sems):
        self.place, self.send_sems, self.recv_sems, self.used, self.open = place, send_sems, recv_sems, 0, []
        self.k, self.z_half = place.at["k"], lax.div(place.at["z"], 4)

    def device(self, dx, dy, dz, k):
        at = self.place.at
        return self.place.device(
            x=lax.rem(at["x"] + 2 * dx, 4),
            y=at["y"] + dy * (1 - 2 * lax.rem(at["y"], 2)),
            z=lax.rem(at["z"] + 4 * dz, 8),
            k=k,
        )

    def peers(self):
        found = [self.device(dx, 0, dz, 1 - self.k) for dx, dz in ((0, 1), (1, 0), (1, 1))]
        return found + [self.device(1, 0, 1, self.k), self.device(0, 1, 0, 1 - self.k)]

    def copy(self, src, dst, device, sem):
        made = pltpu.make_async_remote_copy(
            src_ref=src,
            dst_ref=dst,
            send_sem=self.send_sems.at[self.used],
            recv_sem=self.recv_sems.at[sem],
            device_id=device,
            device_id_type=MESH,
        )
        self.used += 1
        return made

    def send(self, src, dst, device, sem):
        made = self.copy(src, dst, device, sem)
        made.start()
        self.open.append((made, None))

    def send_if(self, when, src, dst, device, sem):
        made = self.copy(src, dst, device, sem)

        @pl.when(when)
        def _():
            made.start()

        self.open.append((made, when))

    def wait(self, dst, sem):
        pltpu.make_async_remote_copy(
            src_ref=dst,
            dst_ref=dst,
            send_sem=self.send_sems.at[0],
            recv_sem=self.recv_sems.at[sem],
            device_id=self.place.other_core(),
            device_id_type=MESH,
        ).wait_recv()

    def wait_if(self, when, dst, sem):
        @pl.when(when)
        def _():
            self.wait(dst, sem)

    def finish(self):
        for made, when in self.open:
            if when is None:
                made.wait_send()
            else:
                pl.when(when)(made.wait_send)


RECVS = 4 + 4 + 4 + 4 + 4 + 4 + 4
SENDS = 4 + 4 + 4 + 3 + 8 + 3


def meets(
    place, group, fetched, edges, shifts, edges_in, shifts_in, source, source_t, block, own_rows, act,
    feat_t, tgt_sum, mixed, src_part, src_in, tgt_in, grads, src_out, steps_out,
    steps_in, src_grad, tgt_grad, greeted,
):
    k, z_half, q = group.k, group.z_half, lax.axis_index("rel")
    scale = EMB ** (-0.5)
    src_feat, tgt_feat, weight, shift, edge_src, edge_tgt, hot, neg, label = fetched
    for ref in (edge_src, edge_tgt, hot, neg, label, shift):
        ref.wait()
    gather_edges(*(ref.here for ref in (edge_src, edge_tgt, hot, neg, label, shift)), edges, shifts)
    for ref in (src_feat, tgt_feat, weight):
        ref.wait()
    feats = jnp.concatenate([src_feat.here[...], tgt_feat.here[...]], 0)
    act[...] = jnp.tanh(dot(feats, weight.here[...]))
    own_rows[...] = act[...].astype(BF16)

    greeted()

    def to_consumers(kind, src_of, dst):
        for dx in range(2):
            for dz in (1, 0):
                args = (src_of(dx), dst, group.device(dx, 0, dz, dx), 4 * kind + 2 * dz + k)
                if dx + dz == 0:
                    group.send_if(k == 1, *args)
                else:
                    group.send(*args)

    src_rows = pl.ds(64 * q, 64)
    to_consumers(2, lambda dx: own_rows.at[0:64], source.at[src_rows])
    to_consumers(0, lambda dx: edges.at[dx], edges_in.at[q])
    to_consumers(1, lambda dx: shifts, shifts_in.at[q])
    for dy, there in ((1, 0), (1, 1), (0, 1 - k)):
        group.send(
            own_rows.at[64:192], block.at[pl.ds(256 * dy + 128 * k, 128)], group.device(0, dy, 0, there), 12 + 2 * dy + k
        )
    block[pl.ds(128 * k, 128)] = own_rows[64:192]

    @pl.when(k == 0)
    def _():
        edges_in[q] = edges[0]
        shifts_in[q] = shifts[...]
        source[src_rows] = own_rows[0:64]

    feat_t[...] = feats.astype(F32).T.astype(BF16)
    tgt_sum[...] = jnp.zeros(tgt_sum.shape, F32)
    mixed[...] = jnp.zeros(mixed.shape, F32)

    def from_producers(kind, dst_of):
        for dz in range(2):
            for there in range(2):
                theirs = lax.rem(z_half + dz, 2) * 2 + there
                args = (dst_of(theirs), 4 * kind + 2 * dz + there)
                if dz + there == 0:
                    group.wait_if(k == 1, *args)
                else:
                    group.wait(*args)

    from_producers(0, lambda g: edges_in.at[g])
    from_producers(1, lambda g: shifts_in.at[g])
    spread_shifts(shifts_in, source)
    from_producers(2, lambda g: source.at[pl.ds(64 * g, 64)])
    source_t[...] = source[...].astype(F32).T.astype(BF16)
    for dy, there in ((0, 1 - k), (1, 0), (1, 1)):
        group.wait(block.at[pl.ds(256 * dy + 128 * there, 128)], 12 + 2 * dy + there)

    def send_tgt(dy, there):
        rows = pl.ds(256 * dy + 128 * there, 128)
        tgt_sum[rows] = scale * tgt_sum[rows]
        group.send(
            tgt_sum.at[rows], tgt_in.at[2 * dy + k], group.device(0, dy, 0, there), 20 + 2 * dy + k
        )

    for s in (1, 0):

        @pl.loop(0, 2)
        def _(turn):
            for g in range(2):
                e = edges_in[2 * turn + g, 16 * s : 16 * s + 16].astype(jnp.int32)
                meet_pair(e, s, 2 * turn + g, z_half, source_t, block, tgt_sum, mixed)

        if s == 1:
            send_tgt(1, 0)
            send_tgt(1, 1)

    high, low = two_terms(mixed[...])
    rows = block[...]
    src_part[...] = scale * (dot(high, rows) + dot(low, rows))
    for part in range(4):
        rows = slice(64 * part, 64 * part + 64)
        src_out[rows], steps_out[part] = narrowed(src_part[rows])
    for dz in (1, 0):
        for there in range(2):
            theirs = lax.rem(z_half + dz, 2) * 2 + there
            device = group.place.device(
                x=lax.rem(place.at["x"] + 2 * k, 4), z=lax.rem(place.at["z"] + 4 * dz, 8), k=there
            )
            slot = 2 * k + dz
            both = (
                (src_out.at[pl.ds(64 * theirs, 64)], src_in.at[slot], device, 16 + slot),
                (steps_out.at[theirs], steps_in.at[slot], device, 24 + slot),
            )
            for args in both:
                if dz + there == 0:
                    group.send_if(k == 1, *args)
                else:
                    group.send(*args)

    @pl.when(k == 0)
    def _():
        src_in[0] = src_out[pl.ds(64 * q, 64)]
        steps_in[0] = steps_out[q]

    send_tgt(0, 1 - k)
    total = scale * tgt_sum[pl.ds(128 * k, 128)]
    for dy, there in ((0, 1 - k), (1, 0), (1, 1)):
        group.wait(tgt_in.at[2 * dy + there], 20 + 2 * dy + there)
        total = total + tgt_in[2 * dy + there]
    tgt_grad[...] = total
    grads[64:192] = (total * (1.0 - act[64:192] * act[64:192])).astype(BF16)
    group.wait_if(k == 1, src_in.at[0], 16)
    group.wait_if(k == 1, steps_in.at[0], 24)
    total = widened(src_in[0], steps_in[0])
    for slot in range(1, 4):
        group.wait(src_in.at[slot], 16 + slot)
        group.wait(steps_in.at[slot], 24 + slot)
        total = total + widened(src_in[slot], steps_in[slot])
    src_grad[...] = total
    grads[0:64] = (total * (1.0 - act[0:64] * act[0:64])).astype(BF16)


def local_sums(half, local, feat_t, grads, src_part):
    lanes = pl.ds(pl.multiple_of(256 * half, 256), 256)
    enc = dot(feat_t[...], grads[:, lanes])
    rel = [src_part[256 + 16 * g : 259 + 16 * g, lanes] for g in range(4)]
    rel = jnp.concatenate(rel + [jnp.zeros((4, 256), F32)], 0)
    for low in range(2):
        cut = slice(128 * low, 128 * low + 128)
        local[pl.ds(half * HALF + low * 96, 96)] = enc[:, cut].reshape(96, 8, 128)
        local[pl.ds(half * HALF + 200 + low * 2, 2)] = rel[:, cut].reshape(2, 8, 128)


def scratch_of_meets():
    return [
        pltpu.VMEM((2, 32, 384), jnp.int16),
        pltpu.VMEM((16, 128), BF16),
        pltpu.VMEM((4, 32, 384), jnp.int16),
        pltpu.VMEM((4, 16, 128), BF16),
        pltpu.VMEM((AUG, EMB), BF16),
        pltpu.VMEM((EMB, AUG), BF16),
        pltpu.VMEM((512, EMB), BF16),
        pltpu.VMEM((192, EMB), BF16),
        pltpu.VMEM((192, EMB), F32),
        pltpu.VMEM((768, 192), BF16),
        pltpu.VMEM((512, EMB), F32),
        pltpu.VMEM((AUG, 512), F32),
        pltpu.VMEM((AUG, EMB), F32),
        pltpu.VMEM((4, 64, EMB), jnp.int16),
        pltpu.VMEM((4, 128, EMB), F32),
        pltpu.VMEM((192, EMB), BF16),
        pltpu.VMEM((256, EMB), jnp.int16),
        pltpu.VMEM((4, 8, 128), F32),
        pltpu.VMEM((4, 8, 128), F32),
    ]


class Fetched:
    def __init__(self, there, here, sem):
        self.here, self.copy = here, pltpu.make_async_copy(there, here, sem)
        self.copy.start()

    def wait(self):
        self.copy.wait()


def kernel(*refs):
    inputs, outputs, (here, meet_buffers, sum_buffers, fetch_sems, *sems) = refs[:9], refs[9:13], refs[13:]
    src_grad, tgt_grad, enc_grad, rel_grad = outputs
    place = Place()
    group = Group(place, sems[0], sems[1])
    barrier = pltpu.get_barrier_semaphore()
    others = [place.along(axis, apart)[1] for axis, n in AXIS.items() for apart in range(1, n)]
    others += [place.other_core()] + group.peers()
    fetched = [None] * 9
    for i in (4, 5, 6, 7, 8, 3, 0, 1, 2):
        fetched[i] = Fetched(inputs[i], here[i], fetch_sems.at[i])
    greet(place, barrier, others)
    meets(
        place, group, fetched, *meet_buffers, src_grad, tgt_grad, lambda: pl.semaphore_wait(barrier, len(others))
    )
    feat_t, src_part, grads = meet_buffers[9], meet_buffers[12], meet_buffers[15]
    wires = Wires(sems[2], sems[3])
    reduce_everywhere(
        place, wires, *sum_buffers, lambda half: local_sums(half, sum_buffers[0], feat_t, grads, src_part)
    )
    tiles_out(sum_buffers[11], enc_grad, rel_grad)
    group.finish()
    wires.finish()


def hand_over(*refs):
    results, outputs, rooms, in_sems, out_sems = refs[:4], refs[4:8], *refs[8:]
    loads = [pltpu.make_async_copy(results[i], rooms[i], in_sems.at[i]) for i in range(4)]
    stores = [pltpu.make_async_copy(rooms[i], outputs[i], out_sems.at[i]) for i in range(4)]
    for load in loads:
        load.start()
    for load, store in zip(loads, stores):
        load.wait()
        store.start()
    for store in stores:
        store.wait()


def shards(*arrays):
    hot = jnp.transpose(arrays[6], (0, 1, 3, 2, 4))
    arrays = arrays[:6] + (hot,) + arrays[7:]
    shapes = ((64, EMB), (128, EMB), (768, EMB), (3, EMB))
    results = pl.pallas_call(
        kernel,
        out_shape=tuple(jax.ShapeDtypeStruct(shape, F32) for shape in shapes),
        in_specs=[pl.BlockSpec(memory_space=pl.ANY)] * 9,
        out_specs=(pl.BlockSpec(memory_space=pltpu.VMEM),) * 4,
        scratch_shapes=[
            [pltpu.VMEM(array.shape, array.dtype) for array in arrays],
            scratch_of_meets(),
            scratch_of_reduce(),
            pltpu.SemaphoreType.DMA((9,)),
            pltpu.SemaphoreType.DMA((SENDS,)),
            pltpu.SemaphoreType.DMA((RECVS,)),
            pltpu.SemaphoreType.DMA((WIRES,)),
            pltpu.SemaphoreType.DMA((WIRES,)),
        ],
        compiler_params=pltpu.CompilerParams(
            collective_id=0, has_side_effects=True, vmem_limit_bytes=56 * 2**20
        ),
    )(*arrays)
    src_grad, tgt_grad, enc_grad, rel_grad = pl.pallas_call(
        hand_over,
        out_shape=tuple(jax.ShapeDtypeStruct(shape, F32) for shape in shapes),
        in_specs=[pl.BlockSpec(memory_space=pl.ANY)] * 4,
        out_specs=(pl.BlockSpec(memory_space=pl.ANY),) * 4,
        scratch_shapes=[
            [pltpu.VMEM(shape, F32) for shape in shapes],
            pltpu.SemaphoreType.DMA((4,)),
            pltpu.SemaphoreType.DMA((4,)),
        ],
        compiler_params=pltpu.CompilerParams(vmem_limit_bytes=56 * 2**20),
    )(*results)
    return src_grad, tgt_grad, rel_grad, enc_grad


def solution(mesh):
    in_specs = (
        P(("bucket", "rel"), None),
        P(("bucket", "rel"), None),
        P(),
        P("rel", None),
        P("bucket", "rel", None, None),
        P("bucket", "rel", None, None),
        P("bucket", "rel", None, None, None),
        P("bucket", "rel", None, None),
        P("bucket", "rel", None, None),
    )
    out_specs = (P(("bucket", "rel"), None), P(("bucket", "rel"), None), P("rel", None), P())
    return jax.shard_map(shards, mesh=mesh, in_specs=in_specs, out_specs=out_specs, check_vma=False)
```

```python
import jax
import jax.numpy as jnp
from jax import lax
from jax.experimental import pallas as pl
from jax.experimental.pallas import tpu as pltpu
from jax.sharding import PartitionSpec as P

EMB = 512
NEG = 128
MEETS = 4
F32 = jnp.float32
BF16 = jnp.bfloat16
MESH = pl.DeviceIdType.MESH
AXIS = {"x": 4, "y": 8, "z": 8}
HALF = 224
PARTS = (("x", "y", "z", 128, 96), ("z", "y", "x", 0, 64), ("y", "z", "x", 64, 64))


def far_first(axis):
    n = AXIS[axis]
    return sorted(range(1, n), key=lambda apart: -min(apart, n - apart))


class Place:
    def __init__(self):
        b, q = lax.axis_index("bucket"), lax.axis_index("rel")
        self.at = {
            "x": lax.div(b, 32),
            "y": lax.rem(b, 8),
            "z": lax.div(q, 2) * 4 + lax.rem(lax.div(b, 8), 4),
            "k": lax.rem(q, 2),
        }

    def device(self, **moved):
        at = dict(self.at, **moved)
        bucket = at["x"] * 32 + lax.rem(at["z"], 4) * 8 + at["y"]
        return bucket, lax.div(at["z"], 4) * 2 + at["k"]

    def along(self, axis, apart):
        there = lax.rem(self.at[axis] + apart, AXIS[axis])
        return there, self.device(**{axis: there})

    def other_core(self):
        return self.device(k=1 - self.at["k"])


class Wires:
    def __init__(self, send_sems, recv_sems):
        self.send_sems, self.recv_sems, self.used, self.open = send_sems, recv_sems, 0, []

    def send(self, src, dst, device):
        copy = pltpu.make_async_remote_copy(
            src_ref=src,
            dst_ref=dst,
            send_sem=self.send_sems.at[self.used],
            recv_sem=self.recv_sems.at[self.used],
            device_id=device,
            device_id_type=MESH,
        )
        copy.start()
        self.used += 1
        self.open.append(copy)
        return copy

    def finish(self):
        for copy in self.open:
            copy.wait_send()


def packed(value):
    most = jnp.max(jnp.max(jnp.abs(value), axis=1, keepdims=True), axis=2, keepdims=True)
    power = jnp.ceil(jnp.log2(jnp.maximum(most, 1e-30)) - 14.99)
    whole = jnp.floor(value * jnp.exp2(-power) + 0.5)
    rows = jnp.broadcast_to(power, (value.shape[0], 1, 16, 128))
    return jnp.concatenate([whole, rows], 1).astype(jnp.int32).astype(jnp.int16)


def unpacked(blocks):
    wide = blocks.astype(jnp.int32).astype(F32)
    last = blocks.shape[1] - 1
    return wide[:, :last] * jnp.exp2(wide[:, last:])


def reduce_everywhere(place, wires, local, pair, mine, full, firsts, seconds, thirds, sums1, sums2, sent, gathered, final, fill):
    at, k = place.at, place.at["k"]
    other = place.other_core()
    copies = []
    for half in (0, HALF):
        local[half + 192 : half + 200] = jnp.zeros((8, 8, 128), F32)
    fill(1 - k)
    for _, _, _, base, size in PARTS:
        size = min(size, 204 - base)
        copies.append(
            wires.send(local.at[pl.ds((1 - k) * HALF + base, size)], pair.at[pl.ds(base, size)], other)
        )
    fill(k)
    mine[pl.ds(204, 20)] = jnp.zeros((20, 8, 128), F32)
    pending1 = []
    for p, (first, _, _, base, size) in enumerate(PARTS):
        copies[p].wait_recv()
        real = min(size, 204 - base)
        mine[pl.ds(base, real)] = local[pl.ds(k * HALF + base, real)] + pair[pl.ds(base, real)]
        block = size // AXIS[first]
        sent[p][...] = packed(mine[pl.ds(base, size)].reshape(AXIS[first], block // 2, 16, 128))
        here = {}
        for apart in far_first(first):
            there, device = place.along(first, apart)
            here[apart] = wires.send(sent[p].at[there], firsts[p].at[apart], device)
        pending1.append(here)
    pending2 = []
    for p, (first, second, _, base, size) in enumerate(PARTS):
        block = size // AXIS[first]
        total = mine[pl.ds(base + at[first] * block, block)]
        for apart in range(1, AXIS[first]):
            pending1[p][apart].wait_recv()
            total = total + unpacked(firsts[p][pl.ds(apart, 1)]).reshape(block, 8, 128)
        sums1[p][...] = total
        small = block // AXIS[second]
        here = {}
        for apart in far_first(second):
            there, device = place.along(second, apart)
            here[apart] = wires.send(sums1[p].at[pl.ds(there * small, small)], seconds[p].at[apart], device)
        pending2.append(here)
    pending3 = []
    for p, (first, second, third, base, size) in enumerate(PARTS):
        small = size // AXIS[first] // AXIS[second]
        total = sums1[p][pl.ds(at[second] * small, small)]
        for apart in range(1, AXIS[second]):
            pending2[p][apart].wait_recv()
            total = total + seconds[p][apart]
        sums2[p][...] = total
        here = {}
        for apart in far_first(third):
            here[apart] = wires.send(sums2[p], thirds[p].at[apart], place.along(third, apart)[1])
        pending3.append(here)
    pending4 = []
    for p, (first, second, third, base, size) in enumerate(PARTS):
        thirds[p][0] = sums2[p][...]
        for apart in range(1, AXIS[third]):
            pending3[p][apart].wait_recv()
        total = 0.0
        for where in range(AXIS[third]):
            total = total + thirds[p][lax.rem(at[third] + AXIS[third] - where, AXIS[third])]
        block = size // AXIS[first]
        small = block // AXIS[second]
        own = k * HALF + base + at[first] * block + at[second] * small
        full[pl.ds(own, small)] = total
        here = []
        for apart in far_first(second):
            piece = full.at[pl.ds(own, small)]
            here.append(wires.send(piece, piece, place.along(second, apart)[1]))
        pending4.append(here)
    pending5, pending6 = [], []
    for p, (first, second, third, base, size) in enumerate(PARTS):
        block = size // AXIS[first]
        for copy in pending4[p]:
            copy.wait_recv()
        own = full[pl.ds(k * HALF + base + at[first] * block, block)].reshape(1, block // 2, 16, 128)
        gathered[p][k, pl.ds(at[first], 1)] = packed(own)
        piece = gathered[p].at[k, at[first]]
        pending5.append(
            {apart: wires.send(piece, piece, place.along(first, apart)[1]) for apart in far_first(first)}
        )
    for p, (first, second, third, base, size) in enumerate(PARTS):
        for apart in reversed(far_first(first)):
            pending5[p][apart].wait_recv()
        piece = gathered[p].at[k]
        pending6.append(wires.send(piece, piece, other))
    for turn, half in enumerate((k, 1 - k)):
        for p, (first, second, third, base, size) in enumerate(PARTS):
            if turn:
                pending6[p].wait_recv()
            final[pl.ds(half * HALF + base, size)] = unpacked(gathered[p][half]).reshape(size, 8, 128)


WIRES = 3 + 17 + 21 + 13 + 21 + 17 + 3


def scratch_of_reduce():
    tile = (8, 128)
    coded = [(AXIS[f], n // AXIS[f] // 2 + 1, 16, 128) for f, s, t, _, n in PARTS]
    firsts = [pltpu.VMEM(shape, jnp.int16) for shape in coded]
    sent = [pltpu.VMEM(shape, jnp.int16) for shape in coded]
    gathered = [pltpu.VMEM((2,) + shape, jnp.int16) for shape in coded]
    small = [n // AXIS[f] // AXIS[s] for f, s, t, _, n in PARTS]
    seconds = [pltpu.VMEM((AXIS[p[1]], m) + tile, F32) for p, m in zip(PARTS, small)]
    thirds = [pltpu.VMEM((AXIS[p[2]], m) + tile, F32) for p, m in zip(PARTS, small)]
    sums1 = [pltpu.VMEM((n // AXIS[f],) + tile, F32) for f, s, t, _, n in PARTS]
    sums2 = [pltpu.VMEM((m,) + tile, F32) for m in small]
    return [
        pltpu.VMEM((2 * HALF,) + tile, F32),
        pltpu.VMEM((HALF,) + tile, F32),
        pltpu.VMEM((HALF,) + tile, F32),
        pltpu.VMEM((2 * HALF,) + tile, F32),
        firsts,
        seconds,
        thirds,
        sums1,
        sums2,
        sent,
        gathered,
        pltpu.VMEM((2 * HALF,) + tile, F32),
    ]


def greet(place, barrier, devices):
    for device in devices:
        pl.semaphore_signal(barrier, inc=1, device_id=device, device_id_type=MESH)


def tiles_out(full, enc_ref, rel_ref):
    g = lax.axis_index("rel")
    for column in range(4):
        half, low = column // 2 * HALF, column % 2
        lanes = pl.ds(column * 128, 128)
        enc_ref[:, lanes] = full[half + low * 96 : half + low * 96 + 96].reshape(768, 128)
        rows = full[half + 200 + low * 2 : half + 202 + low * 2].reshape(16, 128)
        part = jnp.zeros((3, 128), F32)
        for group in range(4):
            part = jnp.where(g == group, rows[group * 3 : group * 3 + 3], part)
        rel_ref[:, lanes] = part


NT = (((1,), (1,)), ((), ()))
ROWS = 768
AUG = 320


def dot(a, b, dims=(((1,), (0,)), ((), ()))):
    return lax.dot_general(a, b, dims, preferred_element_type=F32)


def two_terms(value):
    high = value.astype(BF16)
    return high, (value - high.astype(F32)).astype(BF16)


def is_row(count, width, ids):
    return lax.broadcasted_iota(jnp.int32, (count, width), 0) == ids


def one_hot(count, width, ids):
    return jnp.where(is_row(count, width, ids), 1.0, 0.0).astype(BF16)


def gather_edges(edge_src, edge_tgt, hot, neg, label, shift, edges, shifts):
    edges[...] = jnp.zeros(edges.shape, jnp.int16)
    for pair, slots in enumerate(((0, 1), (3, 2))):
        for s, slot in enumerate(slots):
            row = slice(slot, slot + 1)
            whole = [
                edge_src[0, 0, row, :],
                edge_tgt[0, 0, row, :],
                label[0, 0, row, :],
                hot[0, 0, 1, row, :],
                hot[0, 0, 2, row, :],
            ]
            rows = [part[:, h : h + ROWS // 2] for part in whole for h in (0, ROWS // 2)]
            rows.append(jnp.concatenate([neg[0, 0, row, :], jnp.zeros((1, ROWS // 2 - NEG), jnp.int32)], 1))
            rows.append(jnp.zeros((5, ROWS // 2), jnp.int32))
            edges[pair, 16 * s : 16 * s + 16] = jnp.concatenate(rows, 0).astype(jnp.int16)
    parts = [shift[:, c : c + 128].astype(F32) for c in range(0, EMB, 128)]
    shifts[...] = jnp.concatenate(parts + [jnp.zeros((4, 128), F32)], 0).astype(BF16)


def spread_shifts(shifts, source):
    for g in range(4):
        got = shifts[g].astype(F32)
        rows = jnp.concatenate([got[3 * c : 3 * c + 3] for c in range(4)], 1)
        source[256 + 16 * g : 272 + 16 * g] = jnp.concatenate([rows, jnp.zeros((13, EMB), F32)], 0).astype(BF16)


def meet_pair(e, s, g, z_half, source_t, block, tgt_sum, mixed):
    scale = EMB ** (-0.5)
    rows = [jnp.concatenate([e[i : i + 1], e[i + 1 : i + 2]], 1) for i in range(0, 10, 2)]
    src_ids, tgt_ids, label, which = rows[0], rows[1], rows[2], rows[3] + 2 * rows[4]
    neg_ids = e[10:11, :NEG]
    ends = jnp.concatenate([one_hot(256, ROWS, src_ids), one_hot(64, ROWS, which + 16 * g)], 0)
    query = dot(source_t[...], ends).astype(BF16)
    rows = slice(256 * s, 256 * s + 256)
    prob = 1.0 / (1.0 + jnp.exp(-scale * dot(block[rows], query)))
    times = jnp.sum(
        jnp.where(is_row(256, NEG, neg_ids - 256 * z_half), 1.0, 0.0), axis=1, keepdims=True
    )
    weight = times * (prob * (1.0 / NEG)).astype(BF16).astype(F32)
    weight = weight + jnp.where(
        is_row(256, ROWS, tgt_ids - 256 * z_half), prob - label.astype(F32), 0.0
    )
    high, low = two_terms(weight)
    tgt_sum[rows] += dot(high, query, NT) + dot(low, query, NT)
    mixed[:, rows] += dot(ends, high, NT) + dot(ends, low, NT)


def narrowed(value):
    most = jnp.maximum(jnp.max(jnp.abs(value), axis=0, keepdims=True), 1e-30)
    whole = jnp.floor(value * (32767.0 / most) + 0.5).astype(jnp.int32).astype(jnp.int16)
    step = most * (1.0 / 32767.0)
    rows = [step[:, c : c + 128] for c in range(0, EMB, 128)]
    return whole, jnp.concatenate(rows + [jnp.zeros((4, 128), F32)], 0)


def widened(whole, steps):
    step = jnp.concatenate([steps[c : c + 1] for c in range(4)], 1)
    return whole.astype(jnp.int32).astype(F32) * step


class Group:
    def __init__(self, place, send_sems, recv_sems):
        self.place, self.send_sems, self.recv_sems, self.used, self.open = place, send_sems, recv_sems, 0, []
        self.k, self.z_half = place.at["k"], lax.div(place.at["z"], 4)

    def device(self, dx, dy, dz, k):
        at = self.place.at
        return self.place.device(
            x=lax.rem(at["x"] + 2 * dx, 4),
            y=at["y"] + dy * (1 - 2 * lax.rem(at["y"], 2)),
            z=lax.rem(at["z"] + 4 * dz, 8),
            k=k,
        )

    def peers(self):
        found = [self.device(dx, 0, dz, 1 - self.k) for dx, dz in ((0, 1), (1, 0), (1, 1))]
        return found + [self.device(1, 0, 1, self.k), self.device(0, 1, 0, 1 - self.k)]

    def copy(self, src, dst, device, sem):
        made = pltpu.make_async_remote_copy(
            src_ref=src,
            dst_ref=dst,
            send_sem=self.send_sems.at[self.used],
            recv_sem=self.recv_sems.at[sem],
            device_id=device,
            device_id_type=MESH,
        )
        self.used += 1
        return made

    def send(self, src, dst, device, sem):
        made = self.copy(src, dst, device, sem)
        made.start()
        self.open.append((made, None))

    def send_if(self, when, src, dst, device, sem):
        made = self.copy(src, dst, device, sem)

        @pl.when(when)
        def _():
            made.start()

        self.open.append((made, when))

    def wait(self, dst, sem):
        pltpu.make_async_remote_copy(
            src_ref=dst,
            dst_ref=dst,
            send_sem=self.send_sems.at[0],
            recv_sem=self.recv_sems.at[sem],
            device_id=self.place.other_core(),
            device_id_type=MESH,
        ).wait_recv()

    def wait_if(self, when, dst, sem):
        @pl.when(when)
        def _():
            self.wait(dst, sem)

    def finish(self):
        for made, when in self.open:
            if when is None:
                made.wait_send()
            else:
                pl.when(when)(made.wait_send)


RECVS = 4 + 4 + 4 + 4 + 4 + 4 + 4
SENDS = 4 + 4 + 4 + 3 + 8 + 3


def meets(
    place, group, fetched, edges, shifts, edges_in, shifts_in, source, source_t, block, own_rows, act,
    feat_t, tgt_sum, mixed, src_part, src_in, tgt_in, grads, src_out, steps_out,
    steps_in, src_grad, tgt_grad, greeted,
):
    k, z_half, q = group.k, group.z_half, lax.axis_index("rel")
    scale = EMB ** (-0.5)
    src_feat, tgt_feat, weight, shift, edge_src, edge_tgt, hot, neg, label = fetched
    for ref in (edge_src, edge_tgt, hot, neg, label, shift):
        ref.wait()
    gather_edges(*(ref.here for ref in (edge_src, edge_tgt, hot, neg, label, shift)), edges, shifts)
    for ref in (src_feat, tgt_feat, weight):
        ref.wait()
    feats = jnp.concatenate([src_feat.here[...], tgt_feat.here[...]], 0)
    act[...] = jnp.tanh(dot(feats, weight.here[...]))
    own_rows[...] = act[...].astype(BF16)

    greeted()

    def to_consumers(kind, src_of, dst):
        for dx in range(2):
            for dz in (1, 0):
                args = (src_of(dx), dst, group.device(dx, 0, dz, dx), 4 * kind + 2 * dz + k)
                if dx + dz == 0:
                    group.send_if(k == 1, *args)
                else:
                    group.send(*args)

    src_rows = pl.ds(64 * q, 64)
    to_consumers(2, lambda dx: own_rows.at[0:64], source.at[src_rows])
    to_consumers(0, lambda dx: edges.at[dx], edges_in.at[q])
    to_consumers(1, lambda dx: shifts, shifts_in.at[q])
    for dy, there in ((1, 0), (1, 1), (0, 1 - k)):
        group.send(
            own_rows.at[64:192], block.at[pl.ds(256 * dy + 128 * k, 128)], group.device(0, dy, 0, there), 12 + 2 * dy + k
        )
    block[pl.ds(128 * k, 128)] = own_rows[64:192]

    @pl.when(k == 0)
    def _():
        edges_in[q] = edges[0]
        shifts_in[q] = shifts[...]
        source[src_rows] = own_rows[0:64]

    feat_t[...] = feats.astype(F32).T.astype(BF16)
    tgt_sum[...] = jnp.zeros(tgt_sum.shape, F32)
    mixed[...] = jnp.zeros(mixed.shape, F32)

    def from_producers(kind, dst_of):
        for dz in range(2):
            for there in range(2):
                theirs = lax.rem(z_half + dz, 2) * 2 + there
                args = (dst_of(theirs), 4 * kind + 2 * dz + there)
                if dz + there == 0:
                    group.wait_if(k == 1, *args)
                else:
                    group.wait(*args)

    from_producers(0, lambda g: edges_in.at[g])
    from_producers(1, lambda g: shifts_in.at[g])
    spread_shifts(shifts_in, source)
    from_producers(2, lambda g: source.at[pl.ds(64 * g, 64)])
    source_t[...] = source[...].astype(F32).T.astype(BF16)
    for dy, there in ((0, 1 - k), (1, 0), (1, 1)):
        group.wait(block.at[pl.ds(256 * dy + 128 * there, 128)], 12 + 2 * dy + there)

    def send_tgt(dy, there):
        rows = pl.ds(256 * dy + 128 * there, 128)
        tgt_sum[rows] = scale * tgt_sum[rows]
        group.send(
            tgt_sum.at[rows], tgt_in.at[2 * dy + k], group.device(0, dy, 0, there), 20 + 2 * dy + k
        )

    for s in (1, 0):

        @pl.loop(0, 2)
        def _(turn):
            for g in range(2):
                e = edges_in[2 * turn + g, 16 * s : 16 * s + 16].astype(jnp.int32)
                meet_pair(e, s, 2 * turn + g, z_half, source_t, block, tgt_sum, mixed)

        if s == 1:
            send_tgt(1, 0)
            send_tgt(1, 1)

    high, low = two_terms(mixed[...])
    rows = block[...]
    src_part[...] = scale * (dot(high, rows) + dot(low, rows))
    for part in range(4):
        rows = slice(64 * part, 64 * part + 64)
        src_out[rows], steps_out[part] = narrowed(src_part[rows])
    for dz in (1, 0):
        for there in range(2):
            theirs = lax.rem(z_half + dz, 2) * 2 + there
            device = group.place.device(
                x=lax.rem(place.at["x"] + 2 * k, 4), z=lax.rem(place.at["z"] + 4 * dz, 8), k=there
            )
            slot = 2 * k + dz
            both = (
                (src_out.at[pl.ds(64 * theirs, 64)], src_in.at[slot], device, 16 + slot),
                (steps_out.at[theirs], steps_in.at[slot], device, 24 + slot),
            )
            for args in both:
                if dz + there == 0:
                    group.send_if(k == 1, *args)
                else:
                    group.send(*args)

    @pl.when(k == 0)
    def _():
        src_in[0] = src_out[pl.ds(64 * q, 64)]
        steps_in[0] = steps_out[q]

    send_tgt(0, 1 - k)
    total = scale * tgt_sum[pl.ds(128 * k, 128)]
    for dy, there in ((0, 1 - k), (1, 0), (1, 1)):
        group.wait(tgt_in.at[2 * dy + there], 20 + 2 * dy + there)
        total = total + tgt_in[2 * dy + there]
    tgt_grad[...] = total
    grads[64:192] = (total * (1.0 - act[64:192] * act[64:192])).astype(BF16)
    group.wait_if(k == 1, src_in.at[0], 16)
    group.wait_if(k == 1, steps_in.at[0], 24)
    total = widened(src_in[0], steps_in[0])
    for slot in range(1, 4):
        group.wait(src_in.at[slot], 16 + slot)
        group.wait(steps_in.at[slot], 24 + slot)
        total = total + widened(src_in[slot], steps_in[slot])
    src_grad[...] = total
    grads[0:64] = (total * (1.0 - act[0:64] * act[0:64])).astype(BF16)


def local_sums(half, local, feat_t, grads, src_part):
    lanes = pl.ds(pl.multiple_of(256 * half, 256), 256)
    enc = dot(feat_t[...], grads[:, lanes])
    rel = [src_part[256 + 16 * g : 259 + 16 * g, lanes] for g in range(4)]
    rel = jnp.concatenate(rel + [jnp.zeros((4, 256), F32)], 0)
    for low in range(2):
        cut = slice(128 * low, 128 * low + 128)
        local[pl.ds(half * HALF + low * 96, 96)] = enc[:, cut].reshape(96, 8, 128)
        local[pl.ds(half * HALF + 200 + low * 2, 2)] = rel[:, cut].reshape(2, 8, 128)


def scratch_of_meets():
    return [
        pltpu.VMEM((2, 32, 384), jnp.int16),
        pltpu.VMEM((16, 128), BF16),
        pltpu.VMEM((4, 32, 384), jnp.int16),
        pltpu.VMEM((4, 16, 128), BF16),
        pltpu.VMEM((AUG, EMB), BF16),
        pltpu.VMEM((EMB, AUG), BF16),
        pltpu.VMEM((512, EMB), BF16),
        pltpu.VMEM((192, EMB), BF16),
        pltpu.VMEM((192, EMB), F32),
        pltpu.VMEM((768, 192), BF16),
        pltpu.VMEM((512, EMB), F32),
        pltpu.VMEM((AUG, 512), F32),
        pltpu.VMEM((AUG, EMB), F32),
        pltpu.VMEM((4, 64, EMB), jnp.int16),
        pltpu.VMEM((4, 128, EMB), F32),
        pltpu.VMEM((192, EMB), BF16),
        pltpu.VMEM((256, EMB), jnp.int16),
        pltpu.VMEM((4, 8, 128), F32),
        pltpu.VMEM((4, 8, 128), F32),
    ]


class Fetched:
    def __init__(self, there, here, sem):
        self.here, self.copy = here, pltpu.make_async_copy(there, here, sem)
        self.copy.start()

    def wait(self):
        self.copy.wait()


def kernel(*refs):
    inputs, outputs, (here, meet_buffers, sum_buffers, fetch_sems, *sems) = refs[:9], refs[9:13], refs[13:]
    src_grad, tgt_grad, enc_grad, rel_grad = outputs
    place = Place()
    group = Group(place, sems[0], sems[1])
    barrier = pltpu.get_barrier_semaphore()
    others = [place.along(axis, apart)[1] for axis, n in AXIS.items() for apart in range(1, n)]
    others += [place.other_core()] + group.peers()
    fetched = [None] * 9
    for i in (4, 5, 6, 7, 8, 3, 0, 1, 2):
        fetched[i] = Fetched(inputs[i], here[i], fetch_sems.at[i])
    greet(place, barrier, others)
    meets(
        place, group, fetched, *meet_buffers, src_grad, tgt_grad, lambda: pl.semaphore_wait(barrier, len(others))
    )
    feat_t, src_part, grads = meet_buffers[9], meet_buffers[12], meet_buffers[15]
    wires = Wires(sems[2], sems[3])
    reduce_everywhere(
        place, wires, *sum_buffers, lambda half: local_sums(half, sum_buffers[0], feat_t, grads, src_part)
    )
    tiles_out(sum_buffers[11], enc_grad, rel_grad)
    group.finish()
    wires.finish()


def hand_over(*refs):
    results, outputs, rooms, in_sems, out_sems = refs[:4], refs[4:8], *refs[8:]
    loads = [pltpu.make_async_copy(results[i], rooms[i], in_sems.at[i]) for i in range(4)]
    stores = [pltpu.make_async_copy(rooms[i], outputs[i], out_sems.at[i]) for i in range(4)]
    for load in loads:
        load.start()
    for load, store in zip(loads, stores):
        load.wait()
        store.start()
    for store in stores:
        store.wait()


def shards(*arrays):
    hot = jnp.transpose(arrays[6], (0, 1, 3, 2, 4))
    arrays = arrays[:6] + (hot,) + arrays[7:]
    shapes = ((64, EMB), (128, EMB), (768, EMB), (3, EMB))
    results = pl.pallas_call(
        kernel,
        out_shape=tuple(jax.ShapeDtypeStruct(shape, F32) for shape in shapes),
        in_specs=[pl.BlockSpec(memory_space=pl.ANY)] * 9,
        out_specs=(pl.BlockSpec(memory_space=pltpu.VMEM),) * 4,
        scratch_shapes=[
            [pltpu.VMEM(array.shape, array.dtype) for array in arrays],
            scratch_of_meets(),
            scratch_of_reduce(),
            pltpu.SemaphoreType.DMA((9,)),
            pltpu.SemaphoreType.DMA((SENDS,)),
            pltpu.SemaphoreType.DMA((RECVS,)),
            pltpu.SemaphoreType.DMA((WIRES,)),
            pltpu.SemaphoreType.DMA((WIRES,)),
        ],
        compiler_params=pltpu.CompilerParams(
            collective_id=0, has_side_effects=True, vmem_limit_bytes=56 * 2**20
        ),
    )(*arrays)
    src_grad, tgt_grad, enc_grad, rel_grad = pl.pallas_call(
        hand_over,
        out_shape=tuple(jax.ShapeDtypeStruct(shape, F32) for shape in shapes),
        in_specs=[pl.BlockSpec(memory_space=pl.ANY)] * 4,
        out_specs=(pl.BlockSpec(memory_space=pl.ANY),) * 4,
        scratch_shapes=[
            [pltpu.VMEM(shape, F32) for shape in shapes],
            pltpu.SemaphoreType.DMA((4,)),
            pltpu.SemaphoreType.DMA((4,)),
        ],
        compiler_params=pltpu.CompilerParams(vmem_limit_bytes=56 * 2**20),
    )(*results)
    return src_grad, tgt_grad, rel_grad, enc_grad


def solution(mesh):
    in_specs = (
        P(("bucket", "rel"), None),
        P(("bucket", "rel"), None),
        P(),
        P("rel", None),
        P("bucket", "rel", None, None),
        P("bucket", "rel", None, None),
        P("bucket", "rel", None, None, None),
        P("bucket", "rel", None, None),
        P("bucket", "rel", None, None),
    )
    out_specs = (P(("bucket", "rel"), None), P(("bucket", "rel"), None), P("rel", None), P())
    return jax.shard_map(shards, mesh=mesh, in_specs=in_specs, out_specs=out_specs, check_vma=False)
```
